256 devices in a mesh: seg: 8 (over x, core), blk: 32 (over z, y).
Axes of the slice: x: 4, y: 4, z: 8, core: 2. Of those that a mesh axis runs over, the one named last changes fastest.
Arguments:
- guess_blocks: bfloat16 [8, 32, 512, 512], P('seg', 'blk'), may hold values from -180 to 180, as said below
- onsite_left: bfloat16 [8, 32, 2, 512, 512], P('seg', 'blk'), may hold values from -0.375 to 1.375, as said below
- onsite_right: bfloat16 [8, 32, 2, 512, 512], P('seg', 'blk'), may hold values from -0.375 to 1.375, as said below
- hopping_left: bfloat16 [8, 32, 512, 512], P('seg', 'blk'), may hold values from -0.25 to 0.25
- hopping_right: bfloat16 [8, 32, 512, 512], P('seg', 'blk'), may hold values from -0.25 to 0.25
- sector_dims: int32 [8, 32, 2], P('seg', 'blk'), may hold values from 192 to 512, as said below
- kept_dims: int32 [8, 32], P('seg', 'blk'), may hold values from 64 to 512, as said below
Outputs:
- ground_blocks: float32 [8, 32, 512, 512], P('seg', 'blk')
- energy: float32 [8], P('seg')
- left_environment: bfloat16 [8, 32, 512, 512], P('seg', 'blk')
- right_environment: bfloat16 [8, 32, 512, 512], P('seg', 'blk')
The draws below stay inside these ranges and needn't reach their ends.
Inputs may be any that keep to these rules, and one draw needn't show every extreme that they name: guess_blocks is drawn independently of the other arrays. Each onsite_left[g, s, k] is a symmetric matrix. Each onsite_right[g, s, k] is a symmetric matrix. `sector_dims`: every entry is a multiple of 64; in every segment some sector has 512 live rows and some sector 512 live columns. `kept_dims`: every entry is a multiple of 64; in every segment some sector keeps 512.
All inputs are finite; a program needn't handle non-finite values.
Results may differ from the reference program's by a relative error of at most 0.015.
Values may be sent and summed in bfloat16 or wider, within the bound.
A program may use at most 64 MiB of HBM per device.

```python
import math
import jax
import jax.numpy as jnp
from jax import lax

B = 512
K = 2
ITERS = 4
DIM_STEP = 64
NSEG = 8
S = 32


def symmetric_blocks(samples, lowest):
    clipped = jnp.clip(samples, -6.0, 6.0)
    shaped = (clipped + jnp.swapaxes(clipped, -1, -2)) / math.sqrt(2.0 * B)
    rising = lowest + (1.0 - lowest) * jnp.arange(S, dtype=jnp.float32) / (S - 1)
    identity = jnp.eye(B, dtype=jnp.float32)
    return shaped + rising[None, :, None, None, None] * identity[None, None, None, :, :]


def draw_guess_blocks(key, part):
    key = jax.random.fold_in(key, 11)
    array_shape = (NSEG, S, B, B)
    rising = 1.0 + 2.0 * jnp.arange(S, dtype=jnp.float32) / (S - 1)
    samples = jnp.clip(jax.random.normal(key, array_shape, jnp.float32), -6.0, 6.0)
    return (samples * rising[None, :, None, None]).astype(jnp.bfloat16)


def draw_onsite_left(key, part):
    key = jax.random.fold_in(key, 21)
    array_shape = (NSEG, S, K, B, B)
    samples = jax.random.normal(key, array_shape, jnp.float32)
    return symmetric_blocks(samples, 0.3).astype(jnp.bfloat16)


def draw_onsite_right(key, part):
    key = jax.random.fold_in(key, 22)
    array_shape = (NSEG, S, K, B, B)
    samples = jax.random.normal(key, array_shape, jnp.float32)
    return symmetric_blocks(samples, 0.3).astype(jnp.bfloat16)


def draw_sector_dims(key, part):
    key = jax.random.fold_in(key, 31)
    most_steps = B // DIM_STEP
    least_steps = max(1, most_steps * 3 // 8)
    samples = jax.random.randint(key, (NSEG, S, 2), least_steps, most_steps + 1)
    widest = jax.random.randint(jax.random.fold_in(key, 1), (NSEG, 1, 2), 0, S)
    sectors = jnp.arange(S, dtype=jnp.int32)[None, :, None]
    samples = jnp.where(sectors == widest, most_steps, samples)
    return (samples * DIM_STEP).astype(jnp.int32)


def draw_kept_dims(key, part):
    key = jax.random.fold_in(key, 41)
    most_steps = B // DIM_STEP
    samples = jax.random.randint(key, (NSEG, S), 1, most_steps + 1)
    widest = jax.random.randint(jax.random.fold_in(key, 1), (NSEG, 1), 0, S)
    sectors = jnp.arange(S, dtype=jnp.int32)[None, :]
    samples = jnp.where(sectors == widest, most_steps, samples)
    return (samples * DIM_STEP).astype(jnp.int32)


def steps_of(rng, dims, split, least, top_value):
    level = 1.0
    for position, parts in split:
        heights = jax.random.uniform(jax.random.fold_in(jax.random.fold_in(rng, 6), position), (parts,), jnp.float32, least / len(split), top_value / len(split))
        level = level * jnp.repeat(jnp.exp(heights), dims[position] // parts).reshape((-1,) + (1,) * (len(dims) - 1 - position))
    return level


def centred(rng, dims, scale, limit, cuts=(), kind=jnp.bfloat16):
    gain = steps_of(rng, dims, cuts, -0.22, 0.18) if cuts else 1.0
    values = jax.random.normal(rng, dims, jnp.float32) * scale * gain
    return jnp.minimum(jnp.maximum(values, -limit), limit).astype(kind)


def setup_inputs(seed: int = 0) -> dict:
    seeds = jax.random.split(jax.random.key(seed), 8)
    return {
        "guess_blocks": draw_guess_blocks(jax.random.fold_in(seeds[7], 71), 0),
        "onsite_left": draw_onsite_left(jax.random.fold_in(seeds[7], 71), 0),
        "onsite_right": draw_onsite_right(jax.random.fold_in(seeds[7], 71), 0),
        "hopping_left": centred(seeds[3], (NSEG, S, B, B), B ** -0.5, 0.25, ((0, 8), (1, 32))),
        "hopping_right": centred(seeds[4], (NSEG, S, B, B), B ** -0.5, 0.25, ((0, 8), (1, 32))),
        "sector_dims": draw_sector_dims(jax.random.fold_in(seeds[7], 71), 0),
        "kept_dims": draw_kept_dims(jax.random.fold_in(seeds[7], 71), 0),
    }


def batched(left, right, form):
    return jnp.einsum(form, left.astype(jnp.float32), right.astype(jnp.float32))

def apply_operator(vector, onsite_left, onsite_right, hopping_left, hopping_right, live_mask):
    blocks = vector.astype(jnp.bfloat16)
    summed = jnp.zeros(vector.shape, jnp.float32)
    for term_index in range(K):
        partial_left = batched(onsite_left[:, term_index], blocks, 'sij,sjk->sik').astype(jnp.bfloat16)
        summed = summed + batched(partial_left, onsite_right[:, term_index], 'sij,sjk->sik')
    empty_block = jnp.zeros((1, B, B), jnp.bfloat16)
    following = jnp.concatenate([blocks[1:], empty_block], axis=0)
    partial_next = batched(hopping_left, following, 'sij,sjk->sik').astype(jnp.bfloat16)
    summed = summed + batched(partial_next, hopping_right, 'sij,skj->sik')
    partial_prev = batched(hopping_left, blocks, 'sji,sjk->sik').astype(jnp.bfloat16)
    coupled = batched(partial_prev, hopping_right, 'sij,sjk->sik')
    summed = summed + jnp.concatenate([jnp.zeros((1, B, B), jnp.float32), coupled[:-1]], axis=0)
    return summed * live_mask

def segment_solve(pieces):
    guess_blocks, onsite_left, onsite_right, hopping_left, hopping_right, sector_dims, kept_dims = pieces
    positions = jnp.arange(B, dtype=jnp.int32)
    live_mask = ((positions[None, :, None] < sector_dims[:, 0][:, None, None]) & (positions[None, None, :] < sector_dims[:, 1][:, None, None])).astype(jnp.float32)

    def operator(field):
        return apply_operator(field, onsite_left, onsite_right, hopping_left, hopping_right, live_mask)
    diagonal = jnp.zeros((S, B, B), jnp.float32)
    for term_index in range(K):
        left_diag = jnp.diagonal(onsite_left[:, term_index].astype(jnp.float32), axis1=1, axis2=2)
        right_diag = jnp.diagonal(onsite_right[:, term_index].astype(jnp.float32), axis1=1, axis2=2)
        diagonal = diagonal + left_diag[:, :, None] * right_diag[:, None, :]
    diagonal = diagonal * live_mask
    vector = guess_blocks.astype(jnp.float32) * live_mask
    vector = vector / jnp.sqrt(jnp.sum(vector * vector))
    image = operator(vector)
    energy = jnp.sum(vector * image)
    for iteration in range(ITERS):
        residual = image - energy * vector
        correction = residual / (1.0 + jnp.abs(diagonal - energy))
        applied = operator(correction)
        correlation = jnp.sum(vector * correction)
        weight = jnp.sum(correction * correction)
        cross_term = jnp.sum(vector * applied)
        curvature = jnp.sum(correction * applied)
        span_square = weight - correlation * correlation
        length = jnp.sqrt(span_square)
        off_diagonal = (cross_term - correlation * energy) / length
        lower_value = (curvature - 2.0 * correlation * cross_term + correlation * correlation * energy) / span_square
        half_gap = (energy - lower_value) / 2.0
        radius = jnp.sqrt(half_gap * half_gap + off_diagonal * off_diagonal)
        keep_coef = radius - half_gap
        turn_coef = -off_diagonal
        coef_norm = jnp.sqrt(keep_coef * keep_coef + turn_coef * turn_coef)
        vector = (keep_coef * vector + turn_coef * (correction - correlation * vector) / length) / coef_norm
        image = (keep_coef * image + turn_coef * (applied - correlation * image) / length) / coef_norm
        energy = (energy + lower_value) / 2.0 - radius
    ground = vector * (B * math.sqrt(S))
    final_blocks = vector.astype(jnp.bfloat16)
    kept_mask = ((positions[None, :, None] < kept_dims[:, None, None]) & (positions[None, None, :] < kept_dims[:, None, None])).astype(jnp.float32)
    handoff_scale = S * B * math.sqrt(B)
    left_part = batched(onsite_left[:, 0], final_blocks, 'sij,sjk->sik').astype(jnp.bfloat16)
    outgoing_left = (batched(final_blocks, left_part, 'sji,sjk->sik') * handoff_scale * kept_mask).astype(jnp.bfloat16)
    right_part = batched(final_blocks, onsite_right[:, 0], 'sij,sjk->sik').astype(jnp.bfloat16)
    outgoing_right = (batched(right_part, final_blocks, 'sij,skj->sik') * handoff_scale * kept_mask).astype(jnp.bfloat16)
    return (ground, energy, outgoing_left, outgoing_right)

def reference(guess_blocks, onsite_left, onsite_right, hopping_left, hopping_right, sector_dims, kept_dims):
    ground, energy, outgoing_left, outgoing_right = lax.map(segment_solve, (guess_blocks, onsite_left, onsite_right, hopping_left, hopping_right, sector_dims, kept_dims))
    left_environment = jnp.concatenate([onsite_left[:1, :, 0], outgoing_left[:-1]], axis=0)
    right_environment = jnp.concatenate([outgoing_right[1:], onsite_right[-1:, :, 0]], axis=0)
    return (ground, energy, left_environment, right_environment)
```

```python
import functools
import math

import jax
import jax.numpy as jnp
from jax import lax
from jax.experimental import pallas as pl
from jax.experimental.pallas import tpu as pltpu
from jax.sharding import PartitionSpec as P

ITERS = 4
MESH = pl.DeviceIdType.MESH
F32 = jnp.float32
BF16 = jnp.bfloat16
ROWS = 32
OUTSIDE = 3e38


def dot(a, b):
    return lax.dot_general(a, b, (((1,), (0,)), ((), ())), preferred_element_type=F32)


def dot_nt(a, b):
    return lax.dot_general(a, b, (((1,), (1,)), ((), ())), preferred_element_type=F32)


def fold(x):
    rows, cols = x.shape
    return jnp.sum(x.reshape(rows // 8, 8, cols), axis=0)


def total(x):
    return jnp.sum(jnp.sum(x, axis=0, keepdims=True), axis=1, keepdims=True)


def kernel(
    n, nseg, width,
    guess_h, left_h, right_h, hopl_h, hopr_h, dims, kept,
    ground_o, energy_o, lenv_o, renv_o,
    lv, rv, hl, hlt, hr, gv, diag, vec, img, acc, cb, xr, cs, cr, pp, rm, qq,
    gb, fb, ft, lb, rb, arsrc, arbuf,
    load_sem, xs_sem, xr_sem, cs_sem, cr_sem, as_sem, ar_sem, out_sem, env_s, env_r,
):
    me = lax.axis_index("blk")
    seg = lax.axis_index("seg")
    right, left = lax.rem(me + 1, n), lax.rem(me + n - 1, n)
    half = width // 2
    hs = (pl.ds(0, half), pl.ds(half, half))
    steps = half // ROWS

    loads = [
        pltpu.make_async_copy(src, dst, load_sem.at[i])
        for i, (src, dst) in enumerate(
            ((guess_h, gv), (hopl_h, hl), (hopr_h, hr), (left_h, lv), (right_h, rv))
        )
    ]
    for copy in loads:
        copy.start()
    own_left = pltpu.make_async_copy(left_h.at[0], lenv_o, out_sem.at[1])
    own_right = pltpu.make_async_copy(right_h.at[pl.ds(0, width)], renv_o, out_sem.at[2])

    barrier = pltpu.get_barrier_semaphore()

    def greet(d, _):
        pl.semaphore_signal(
            barrier, inc=1, device_id={"blk": lax.rem(me + d, n)}, device_id_type=MESH
        )
        return 0

    lax.fori_loop(1, n, greet, 0)
    for d in (1, nseg - 1):
        pl.semaphore_signal(
            barrier, inc=1, device_id={"seg": lax.rem(seg + d, nseg)}, device_id_type=MESH
        )

    @pl.when(seg == 0)
    def _():
        own_left.start()

    @pl.when(seg == nseg - 1)
    def _():
        own_right.start()

    live_rows, live_cols = dims[0, 0], dims[0, 1]

    def live(row0, h, rows):
        i = lax.broadcasted_iota(jnp.int32, (rows, half), 0) + row0
        j = lax.broadcasted_iota(jnp.int32, (rows, half), 1) + h * half
        return (i < live_rows) & (j < live_cols)

    def x_copy(par, h, rc):
        rows = pl.ds(rc * half, half)
        return pltpu.make_async_remote_copy(
            src_ref=cb.at[h, rows], dst_ref=xr.at[par, h, rows],
            send_sem=xs_sem.at[h], recv_sem=xr_sem.at[par, h],
            device_id={"blk": left}, device_id_type=MESH,
        )

    def x_whole(par, h):
        return pltpu.make_async_remote_copy(
            src_ref=cb.at[h], dst_ref=xr.at[par, h],
            send_sem=xs_sem.at[h], recv_sem=xr_sem.at[par, h],
            device_id={"blk": left}, device_id_type=MESH,
        )

    def c_copy(par, h):
        return pltpu.make_async_remote_copy(
            src_ref=cs.at[h], dst_ref=cr.at[par, h],
            send_sem=cs_sem.at[h], recv_sem=cr_sem.at[par, h],
            device_id={"blk": right}, device_id_type=MESH,
        )

    loads[0].wait()
    zero_sum = jnp.zeros((8, half), F32)

    def first(h):
        def step(i, weight):
            row0 = pl.multiple_of(i * ROWS, ROWS)
            rows = pl.ds(row0, ROWS)
            c = jnp.where(live(row0, h, ROWS), gv[rows, hs[h]].astype(F32), 0.0)
            cb[h, rows] = c.astype(BF16)
            vec[h, rows] = jnp.zeros((ROWS, half), F32)
            img[h, rows] = jnp.zeros((ROWS, half), F32)
            return weight + fold(c * c)

        return step

    weight0 = zero_sum
    for h in (0, 1):
        weight0 = lax.fori_loop(0, width // ROWS, first(h), weight0)

    pl.semaphore_wait(barrier, n - 1 + 2)
    for h in (0, 1):
        for rc in (0, 1):
            x_copy(0, h, rc).start()

    loads[1].wait()

    @pl.when(me == n - 1)
    def _():
        hl[...] = jnp.zeros_like(hl)

    hlt[...] = hl[...].T
    loads[2].wait()

    def couple(par, halves):
        for h in (0, 1):
            rm[:, hs[h]] = dot(hlt[...], cb[h]).astype(BF16)
        for h in halves:
            cs[h] = dot(rm[...], hr[:, hs[h]]).astype(BF16)
            c_copy(par, h).start()

    def onsite():
        for k in (0, 1):
            for h in (0, 1):
                pp[:, pl.ds(k * width + h * half, half)] = dot(lv[k], cb[h]).astype(BF16)
        for h in (0, 1):
            acc[h] = dot(pp[...], rv[:, hs[h]])

    def ar_whole(par):
        return pltpu.make_async_remote_copy(
            src_ref=arbuf.at[par, pl.ds(0, n - 1)], dst_ref=arbuf.at[par, pl.ds(0, n - 1)],
            send_sem=as_sem.at[par], recv_sem=ar_sem.at[par],
            device_id={"blk": right}, device_id_type=MESH,
        )

    lane = lax.broadcasted_iota(jnp.int32, (1, 128), 1)

    def first_half(par, corr, weight, cross):
        x_whole(par, 0).wait_recv()
        qq[...] = dot(hl[...], xr[par, 0]).astype(BF16)
        c_copy(par, 1).wait_recv()
        curv = jnp.zeros((8, half), F32)
        for h in (0, 1):
            part = dot_nt(qq[...], hr[hs[h], hs[0]])
            local = acc[h]
            terms = local + 2.0 * part
            if h == 1:
                terms = terms + 2.0 * cr[par, 1].astype(F32)
            curv = curv + fold(cb[h].astype(F32) * terms)
            acc[h] = local + part
        sums = [total(s) for s in (corr, weight, cross, curv)]
        row = jnp.zeros((1, 128), F32)
        for k in range(4):
            row = jnp.where(lane == k, sums[k], row)
        arsrc[par, 0:1] = row
        arbuf[par, n - 1 : n] = row
        for d in range(1, n):
            pltpu.make_async_remote_copy(
                src_ref=arsrc.at[par, pl.ds(0, 1)], dst_ref=arbuf.at[par, pl.ds(d - 1, 1)],
                send_sem=as_sem.at[par], recv_sem=ar_sem.at[par],
                device_id={"blk": lax.rem(me + d, n)}, device_id_type=MESH,
            ).start()

    def second_half(par):
        x_whole(par, 1).wait_recv()
        qq[...] = dot(hl[...], xr[par, 1]).astype(BF16)
        for h in (0, 1):
            acc[h] = acc[h] + dot_nt(qq[...], hr[hs[h], hs[1]])
        c_copy(par, 0).wait_recv()

    def coefficients(par, start, energy):
        whole = ar_whole(par)
        whole.wait_recv()
        tot = jnp.sum(arbuf[par], axis=0, keepdims=True)
        corr, weight, cross, curv = (
            jnp.sum(jnp.where(lane == k, tot, 0.0), axis=1, keepdims=True) for k in range(4)
        )
        whole.wait_send()
        span = weight - corr * corr
        length = jnp.sqrt(span)
        off = (cross - corr * energy) / length
        lower = (curv - 2.0 * corr * cross + corr * corr * energy) / span
        gap = (energy - lower) / 2.0
        radius = jnp.sqrt(gap * gap + off * off)
        keep = radius - gap
        turn = -off
        norm = jnp.sqrt(keep * keep + turn * turn)
        scale = turn / (length * norm)
        a = keep / norm - scale * corr
        new = (energy + lower) / 2.0 - radius
        if start is None:
            return a, scale, new
        a = jnp.where(start, 0.0, a)
        scale = jnp.where(start, 1.0 / length, scale)
        new = jnp.where(start, lower, new)
        return a, scale, new

    def sent(halves_x, halves_c):
        for h in halves_x:
            x_whole(0, h).wait_send()
        for h in halves_c:
            c_copy(0, h).wait_send()

    def prepare():
        i = lax.broadcasted_iota(jnp.int32, (128, 128), 0)
        eye = i == lax.broadcasted_iota(jnp.int32, (128, 128), 1)
        for h in (0, 1):
            cols = [
                [
                    jnp.sum(
                        jnp.where(
                            eye,
                            rv[pl.ds(k * width + b, 128), pl.ds(b, 128)].astype(F32),
                            0.0,
                        ),
                        axis=0,
                        keepdims=True,
                    )
                    for b in range(h * half, (h + 1) * half, 128)
                ]
                for k in (0, 1)
            ]
            cols = [jnp.concatenate(c, axis=1) for c in cols]
            for b in range(0, width, 128):
                value = jnp.zeros((128, half), F32)
                for k in (0, 1):
                    block = lv[k, pl.ds(b, 128), pl.ds(b, 128)].astype(F32)
                    col = jnp.sum(jnp.where(eye, block, 0.0), axis=1, keepdims=True)
                    value = value + col * cols[k]
                diag[h, pl.ds(b, 128)] = jnp.where(live(b, h, 128), value, OUTSIDE)

    def update(par, last, a, scale, energy):
        def chunk(q, sums):
            h, rc = q // 2, lax.rem(q, 2)

            def step(i, sums):
                corr, weight, cross = sums
                rows = pl.ds(pl.multiple_of(rc * half + i * ROWS, ROWS), ROWS)
                c = cb[h, rows].astype(F32)
                v = a * vec[h, rows] + scale * c
                m = a * img[h, rows] + scale * (acc[h, rows] + cr[par, h, rows].astype(F32))
                vec[h, rows] = v
                img[h, rows] = m
                d = diag[h, rows]
                w = 1.0 + jnp.abs(d - energy)
                inv = pl.reciprocal(w, approx=True)
                inv = inv * (2.0 - w * inv)
                new = jnp.where(d < OUTSIDE, (m - energy * v) * inv, 0.0).astype(BF16)
                cb[h, rows] = new
                c = new.astype(F32)
                return corr + fold(v * c), weight + fold(c * c), cross + fold(m * c)

            sums = lax.fori_loop(0, steps, step, sums)

            @pl.when(jnp.logical_or(h == 0, jnp.logical_not(last)))
            def _():
                x_copy(1 - par, h, rc).start()

            return sums

        return lax.fori_loop(0, 4, chunk, (zero_sum, zero_sum, zero_sum))

    couple(0, (1, 0))
    loads[3].wait()
    loads[4].wait()
    prepare()

    def iteration(t, carry):
        energy, corr, weight, cross = carry
        par = lax.rem(t, 2)

        @pl.when(t > 0)
        def _():
            couple(par, (1, 0))

        onsite()
        first_half(par, corr, weight, cross)
        second_half(par)
        a, scale, energy = coefficients(par, t == 0, energy)
        sent((0, 1), (0, 1))
        return (energy,) + update(par, t == ITERS - 1, a, scale, energy)

    carry = (jnp.zeros((1, 1), F32), zero_sum, weight0, zero_sum)
    energy, corr, weight, cross = lax.fori_loop(0, ITERS, iteration, carry)
    par = ITERS % 2
    couple(par, (1,))
    onsite()
    first_half(par, corr, weight, cross)
    a, scale, energy = coefficients(par, None, energy)
    energy_o[0] = jnp.sum(energy)

    for h in (0, 1):
        def step(i, _):
            rows = pl.ds(pl.multiple_of(i * ROWS, ROWS), ROWS)
            v = a * vec[h, rows] + scale * cb[h, rows].astype(F32)
            gb[rows, hs[h]] = v * (width * math.sqrt(n))
            fb[rows, hs[h]] = v.astype(BF16)
            return 0

        lax.fori_loop(0, width // ROWS, step, 0)
    ground_copy = pltpu.make_async_copy(gb, ground_o, out_sem.at[0])
    ground_copy.start()

    handoff = n * width * math.sqrt(width)
    size = kept[0, 0]
    i = lax.broadcasted_iota(jnp.int32, (width, half), 0)
    j = lax.broadcasted_iota(jnp.int32, (width, half), 1)

    def kept_part(x, h):
        return jnp.where((i < size) & (j + h * half < size), x * handoff, 0.0).astype(BF16)

    to_next = pltpu.make_async_remote_copy(
        src_ref=lb, dst_ref=lenv_o, send_sem=env_s.at[0], recv_sem=env_r.at[0],
        device_id={"seg": lax.rem(seg + 1, nseg)}, device_id_type=MESH,
    )
    to_previous = pltpu.make_async_remote_copy(
        src_ref=rb, dst_ref=renv_o, send_sem=env_s.at[1], recv_sem=env_r.at[1],
        device_id={"seg": lax.rem(seg + nseg - 1, nseg)}, device_id_type=MESH,
    )
    for h in (0, 1):
        rm[:, hs[h]] = dot(fb[...], rv[pl.ds(0, width), hs[h]]).astype(BF16)
    for h in (0, 1):
        rb[:, hs[h]] = kept_part(dot_nt(rm[...], fb[hs[h], :]), h)

    @pl.when(seg > 0)
    def _():
        to_previous.start()

    ft[...] = fb[...].T
    for h in (0, 1):
        rm[:, hs[h]] = dot(lv[0], fb[:, hs[h]]).astype(BF16)
    for h in (0, 1):
        lb[:, hs[h]] = kept_part(dot(ft[...], rm[:, hs[h]]), h)

    @pl.when(seg < nseg - 1)
    def _():
        to_next.start()

    sent((0,), (1,))
    ground_copy.wait()

    @pl.when(seg > 0)
    def _():
        to_previous.wait_send()
        to_next.wait_recv()

    @pl.when(seg < nseg - 1)
    def _():
        to_next.wait_send()
        to_previous.wait_recv()

    @pl.when(seg == 0)
    def _():
        own_left.wait()

    @pl.when(seg == nseg - 1)
    def _():
        own_right.wait()


def per_device(
    guess_blocks, onsite_left, onsite_right, hopping_left, hopping_right, sector_dims, kept_dims
):
    n, nseg = lax.axis_size("blk"), lax.axis_size("seg")
    width = guess_blocks.shape[-1]
    half = width // 2
    square, halves = (width, width), (2, width, half)
    hbm = pl.BlockSpec(memory_space=pltpu.HBM)
    smem = pl.BlockSpec(memory_space=pltpu.SMEM)
    dma = pltpu.SemaphoreType.DMA
    scratch = [
        pltpu.VMEM((2,) + square, BF16),
        pltpu.VMEM((2 * width, width), BF16),
        pltpu.VMEM(square, BF16),
        pltpu.VMEM(square, BF16),
        pltpu.VMEM(square, BF16),
        pltpu.VMEM(square, BF16),
        pltpu.VMEM(halves, F32),
        pltpu.VMEM(halves, F32),
        pltpu.VMEM(halves, F32),
        pltpu.VMEM(halves, F32),
        pltpu.VMEM(halves, BF16),
        pltpu.VMEM((2,) + halves, BF16),
        pltpu.VMEM(halves, BF16),
        pltpu.VMEM((2,) + halves, BF16),
        pltpu.VMEM((width, 2 * width), BF16),
        pltpu.VMEM(square, BF16),
        pltpu.VMEM((width, half), BF16),
        pltpu.VMEM(square, F32),
        pltpu.VMEM(square, BF16),
        pltpu.VMEM(square, BF16),
        pltpu.VMEM(square, BF16),
        pltpu.VMEM(square, BF16),
        pltpu.VMEM((2, 8, 128), F32),
        pltpu.VMEM((2, n, 128), F32),
        dma((5,)), dma((2,)), dma((2, 2)), dma((2,)), dma((2, 2)), dma((2,)), dma((2,)),
        dma((3,)), dma((2,)), dma((2,)),
    ]
    ground, energy, lenv, renv = pl.pallas_call(
        functools.partial(kernel, n, nseg, width),
        out_shape=(
            jax.ShapeDtypeStruct(square, F32),
            jax.ShapeDtypeStruct((1,), F32),
            jax.ShapeDtypeStruct(square, BF16),
            jax.ShapeDtypeStruct(square, BF16),
        ),
        in_specs=[hbm] * 5 + [smem] * 2,
        out_specs=(hbm, smem, hbm, hbm),
        scratch_shapes=scratch,
        compiler_params=pltpu.CompilerParams(
            collective_id=0, has_side_effects=True, vmem_limit_bytes=60 * 2**20
        ),
    )(
        guess_blocks[0, 0],
        onsite_left[0, 0],
        onsite_right[0, 0].reshape(2 * width, width),
        hopping_left[0, 0],
        hopping_right[0, 0],
        sector_dims[0],
        kept_dims,
    )
    return ground[None, None], energy, lenv[None, None], renv[None, None]


def solution(mesh):
    in_specs = (
        P("seg", "blk", None, None),
        P("seg", "blk", None, None, None),
        P("seg", "blk", None, None, None),
        P("seg", "blk", None, None),
        P("seg", "blk", None, None),
        P("seg", "blk", None),
        P("seg", "blk"),
    )
    out_specs = (
        P("seg", "blk", None, None),
        P("seg"),
        P("seg", "blk", None, None),
        P("seg", "blk", None, None),
    )
    return jax.shard_map(
        per_device, mesh=mesh, in_specs=in_specs, out_specs=out_specs, check_vma=False
    )
```

```python
import functools
import math

import jax
import jax.numpy as jnp
from jax import lax
from jax.experimental import pallas as pl
from jax.experimental.pallas import tpu as pltpu
from jax.sharding import PartitionSpec as P

ITERS = 4
MESH = pl.DeviceIdType.MESH
F32 = jnp.float32
BF16 = jnp.bfloat16
ROWS = 32
OUTSIDE = 3e38


def dot(a, b):
    return lax.dot_general(a, b, (((1,), (0,)), ((), ())), preferred_element_type=F32)


def dot_nt(a, b):
    return lax.dot_general(a, b, (((1,), (1,)), ((), ())), preferred_element_type=F32)


def fold(x):
    rows, cols = x.shape
    return jnp.sum(x.reshape(rows // 8, 8, cols), axis=0)


def total(x):
    return jnp.sum(jnp.sum(x, axis=0, keepdims=True), axis=1, keepdims=True)


def kernel(
    n, nseg, width,
    guess_h, left_h, right_h, hopl_h, hopr_h, dims_h, kept_h,
    ground_o, energy_o, lenv_o, renv_o,
    lv, rv, hl, hlt, hrc, gv, diag, vec, img, acc, cb, xr, cs, cr, pp, rm, qq,
    ff, tt, xx, yy, lsend, rsend, lrecv, rrecv, ratio, ratio_in, arsrc, arbuf, dims, kept,
    load_sem, xs_sem, xr_sem, cs_sem, cr_sem, as_sem, ar_sem, out_sem, env_s, env_r,
    ratio_s, ratio_r,
):
    me = lax.axis_index("blk")
    seg = lax.axis_index("seg")
    right, left = lax.rem(me + 1, n), lax.rem(me + n - 1, n)
    half = width // 2
    hs = (pl.ds(0, half), pl.ds(half, half))
    steps = half // ROWS

    loads = [
        pltpu.make_async_copy(src, dst, load_sem.at[i])
        for i, (src, dst) in enumerate(
            (
                (dims_h, dims),
                (guess_h, gv),
                (hopl_h, hl),
                (hopr_h.at[:, hs[0]], hrc.at[0]),
                (hopr_h.at[:, hs[1]], hrc.at[1]),
                (left_h, lv),
                (right_h, rv),
                (kept_h, kept),
            )
        )
    ]
    for copy in loads:
        copy.start()
    own_left = pltpu.make_async_copy(left_h.at[0], lenv_o, out_sem.at[1])
    own_right = pltpu.make_async_copy(right_h.at[pl.ds(0, width)], renv_o, out_sem.at[2])

    barrier = pltpu.get_barrier_semaphore()

    def greet(d, _):
        pl.semaphore_signal(
            barrier, inc=1, device_id={"blk": lax.rem(me + d, n)}, device_id_type=MESH
        )
        return 0

    lax.fori_loop(1, n, greet, 0)
    for d in (1, nseg - 1):
        pl.semaphore_signal(
            barrier, inc=1, device_id={"seg": lax.rem(seg + d, nseg)}, device_id_type=MESH
        )

    @pl.when(seg == 0)
    def _():
        own_left.start()

    @pl.when(seg == nseg - 1)
    def _():
        own_right.start()

    loads[0].wait()
    live_rows, live_cols = dims[0, 0], dims[0, 1]

    def live(row0, h, rows):
        i = lax.broadcasted_iota(jnp.int32, (rows, half), 0) + row0
        j = lax.broadcasted_iota(jnp.int32, (rows, half), 1) + h * half
        return (i < live_rows) & (j < live_cols)

    def x_copy(par, h, rc):
        rows = pl.ds(rc * half, half)
        return pltpu.make_async_remote_copy(
            src_ref=cb.at[h, rows], dst_ref=xr.at[par, h, rows],
            send_sem=xs_sem.at[h], recv_sem=xr_sem.at[par, h],
            device_id={"blk": left}, device_id_type=MESH,
        )

    def x_whole(par, h):
        return pltpu.make_async_remote_copy(
            src_ref=cb.at[h], dst_ref=xr.at[par, h],
            send_sem=xs_sem.at[h], recv_sem=xr_sem.at[par, h],
            device_id={"blk": left}, device_id_type=MESH,
        )

    def c_copy(par, h):
        return pltpu.make_async_remote_copy(
            src_ref=cs.at[h], dst_ref=cr.at[par, h],
            send_sem=cs_sem.at[h], recv_sem=cr_sem.at[par, h],
            device_id={"blk": right}, device_id_type=MESH,
        )

    loads[1].wait()
    zero_sum = jnp.zeros((8, half), F32)

    def first(h):
        def step(i, weight):
            row0 = pl.multiple_of(i * ROWS, ROWS)
            rows = pl.ds(row0, ROWS)
            c = jnp.where(live(row0, h, ROWS), gv[rows, hs[h]].astype(F32), 0.0)
            cb[h, rows] = c.astype(BF16)
            return weight + fold(c * c)

        return step

    weight0 = zero_sum
    for h in (0, 1):
        weight0 = lax.fori_loop(0, width // ROWS, first(h), weight0)

    pl.semaphore_wait(barrier, n - 1 + 2)
    for h in (0, 1):
        for rc in (0, 1):
            x_copy(0, h, rc).start()

    loads[2].wait()

    @pl.when(me == n - 1)
    def _():
        hl[...] = jnp.zeros_like(hl)

    hlt[...] = hl[...].T
    loads[3].wait()
    loads[4].wait()

    def couple(par, halves):
        for h in (0, 1):
            rm[:, hs[h]] = dot(hlt[...], cb[h]).astype(BF16)
        for h in halves:
            cs[h] = dot(rm[...], hrc[h]).astype(BF16)
            c_copy(par, h).start()

    def onsite():
        for k in (0, 1):
            for h in (0, 1):
                pp[:, pl.ds(k * width + h * half, half)] = dot(lv[k], cb[h]).astype(BF16)
        for h in (0, 1):
            acc[h] = dot(pp[...], rv[:, hs[h]])

    def ar_whole(par):
        return pltpu.make_async_remote_copy(
            src_ref=arbuf.at[par, pl.ds(0, n - 1)], dst_ref=arbuf.at[par, pl.ds(0, n - 1)],
            send_sem=as_sem.at[par], recv_sem=ar_sem.at[par],
            device_id={"blk": right}, device_id_type=MESH,
        )

    lane = lax.broadcasted_iota(jnp.int32, (1, 128), 1)

    def first_half(par, f, corr, weight, cross):
        x_whole(par, f).wait_recv()
        qq[...] = dot(hl[...], xr[par, f]).astype(BF16)
        c_copy(par, 1 - f).wait_recv()
        curv = jnp.zeros((8, half), F32)
        for h in (f, 1 - f):
            part = dot_nt(qq[...], hrc[f, pl.ds(h * half, half)])
            local = acc[h]
            terms = local + 2.0 * part
            if h is not f:
                terms = terms + 2.0 * cr[par, h].astype(F32)
            curv = curv + fold(cb[h].astype(F32) * terms)
            acc[h] = local + part
        sums = [total(s) for s in (corr, weight, cross, curv)]
        row = jnp.zeros((1, 128), F32)
        for k in range(4):
            row = jnp.where(lane == k, sums[k], row)
        arsrc[par, 0:1] = row
        arbuf[par, n - 1 : n] = row
        for d in range(1, n):
            pltpu.make_async_remote_copy(
                src_ref=arsrc.at[par, pl.ds(0, 1)], dst_ref=arbuf.at[par, pl.ds(d - 1, 1)],
                send_sem=as_sem.at[par], recv_sem=ar_sem.at[par],
                device_id={"blk": lax.rem(me + d, n)}, device_id_type=MESH,
            ).start()

    def second_half(par, f):
        x_whole(par, 1 - f).wait_recv()
        qq[...] = dot(hl[...], xr[par, 1 - f]).astype(BF16)
        for h in (0, 1):
            acc[h] = acc[h] + dot_nt(qq[...], hrc[1 - f, hs[h]])

    def coefficients(par, start, energy):
        whole = ar_whole(par)
        whole.wait_recv()
        tot = jnp.sum(arbuf[par], axis=0, keepdims=True)
        corr, weight, cross, curv = (
            jnp.sum(jnp.where(lane == k, tot, 0.0), axis=1, keepdims=True) for k in range(4)
        )
        whole.wait_send()
        span = weight - corr * corr
        length = jnp.sqrt(span)
        off = (cross - corr * energy) / length
        lower = (curv - 2.0 * corr * cross + corr * corr * energy) / span
        gap = (energy - lower) / 2.0
        radius = jnp.sqrt(gap * gap + off * off)
        keep = radius - gap
        turn = -off
        norm = jnp.sqrt(keep * keep + turn * turn)
        scale = turn / (length * norm)
        a = keep / norm - scale * corr
        new = (energy + lower) / 2.0 - radius
        if start is None:
            return a, scale, new
        a = jnp.where(start, 0.0, a)
        scale = jnp.where(start, 1.0 / length, scale)
        new = jnp.where(start, lower, new)
        return a, scale, new

    def prepare():
        vec[...] = jnp.zeros_like(vec)
        img[...] = jnp.zeros_like(img)
        i = lax.broadcasted_iota(jnp.int32, (128, 128), 0)
        eye = i == lax.broadcasted_iota(jnp.int32, (128, 128), 1)
        for h in (0, 1):
            cols = [
                [
                    jnp.sum(
                        jnp.where(
                            eye,
                            rv[pl.ds(k * width + b, 128), pl.ds(b, 128)].astype(F32),
                            0.0,
                        ),
                        axis=0,
                        keepdims=True,
                    )
                    for b in range(h * half, (h + 1) * half, 128)
                ]
                for k in (0, 1)
            ]
            cols = [jnp.concatenate(c, axis=1) for c in cols]
            for b in range(0, width, 128):
                value = jnp.zeros((128, half), F32)
                for k in (0, 1):
                    block = lv[k, pl.ds(b, 128), pl.ds(b, 128)].astype(F32)
                    col = jnp.sum(jnp.where(eye, block, 0.0), axis=1, keepdims=True)
                    value = value + col * cols[k]
                diag[h, pl.ds(b, 128)] = jnp.where(live(b, h, 128), value, OUTSIDE)

    def update(par, f, last, a, scale, energy):
        sums = (zero_sum, zero_sum, zero_sum)
        for h in (1 - f, f):
            if h is f:
                c_copy(par, f).wait_recv()

            def chunk(rc, sums, h=h):
                def step(i, sums):
                    corr, weight, cross = sums
                    rows = pl.ds(pl.multiple_of(rc * half + i * ROWS, ROWS), ROWS)
                    c = cb[h, rows].astype(F32)
                    v = a * vec[h, rows] + scale * c
                    m = a * img[h, rows] + scale * (acc[h, rows] + cr[par, h, rows].astype(F32))
                    vec[h, rows] = v
                    img[h, rows] = m
                    d = diag[h, rows]
                    w = 1.0 + jnp.abs(d - energy)
                    inv = pl.reciprocal(w, approx=True)
                    inv = inv * (2.0 - w * inv)
                    new = jnp.where(d < OUTSIDE, (m - energy * v) * inv, 0.0).astype(BF16)
                    cb[h, rows] = new
                    c = new.astype(F32)
                    return corr + fold(v * c), weight + fold(c * c), cross + fold(m * c)

                sums = lax.fori_loop(0, steps, step, sums)
                if h is not f:
                    x_copy(1 - par, h, rc).start()
                else:

                    @pl.when(jnp.logical_not(last))
                    def _():
                        x_copy(1 - par, h, rc).start()

                return sums

            sums = lax.fori_loop(0, 2, chunk, sums)
        return sums

    couple(0, (1, 0))
    loads[5].wait()
    loads[6].wait()
    prepare()

    def iteration(t, carry):
        energy, corr, weight, cross = carry
        par = lax.rem(t, 2)
        f = par

        @pl.when(t > 0)
        def _():
            for h in (0, 1):
                c_copy(0, h).wait_send()
            couple(par, (1 - f, f))

        onsite()
        first_half(par, f, corr, weight, cross)
        second_half(par, f)
        a, scale, energy = coefficients(par, t == 0, energy)
        for h in (0, 1):
            x_whole(0, h).wait_send()
        return (energy,) + update(par, f, t == ITERS - 1, a, scale, energy)

    carry = (jnp.zeros((1, 1), F32), zero_sum, weight0, zero_sum)
    energy, corr, weight, cross = lax.fori_loop(0, ITERS, iteration, carry)
    par = ITERS % 2
    f = par
    for h in (0, 1):
        c_copy(0, h).wait_send()
    couple(par, (1 - f,))
    onsite()

    loads[7].wait()
    size = kept[0, 0]
    quarters = ((0, 0), (1, 0), (1, 1))

    def env_copy(which, part):
        src, dst = ((lsend, lrecv), (rsend, rrecv))[which]
        other = lax.rem(seg + (1, nseg - 1)[which], nseg)
        if part is not None:
            src, dst = src.at[part], dst.at[part]
        return pltpu.make_async_remote_copy(
            src_ref=src, dst_ref=dst, send_sem=env_s.at[which], recv_sem=env_r.at[which],
            device_id={"seg": other}, device_id_type=MESH,
        )

    def ratio_copy(which):
        other = lax.rem(seg + (1, nseg - 1)[which], nseg)
        return pltpu.make_async_remote_copy(
            src_ref=ratio.at[pl.ds(0, 1)], dst_ref=ratio_in.at[which, pl.ds(0, 1)],
            send_sem=ratio_s.at[which], recv_sem=ratio_r.at[which],
            device_id={"seg": other}, device_id_type=MESH,
        )

    sends = (seg < nseg - 1, seg > 0)
    i = lax.broadcasted_iota(jnp.int32, (half, half), 0)
    j = lax.broadcasted_iota(jnp.int32, (half, half), 1)
    first, second = pl.ds(0, width), pl.ds(width, width)
    for h in (0, 1):
        ff[:, hs[h]] = cb[h]
        ff[:, pl.ds(width + h * half, half)] = vec[h].astype(BF16)
    tt[:, first] = ff[:, first].T
    tt[:, second] = ff[:, second].T
    for h in (0, 1):
        xx[first, hs[h]] = dot(lv[0], ff[:, pl.ds(width + h * half, half)]).astype(BF16)
        yy[:, hs[h]] = dot(ff[:, second], rv[first, hs[h]]).astype(BF16)
    xx[second, :] = pp[:, first]
    for h in (0, 1):
        yy[:, pl.ds(width + h * half, half)] = dot(ff[:, first], rv[first, hs[h]]).astype(BF16)
    everything = pl.ds(0, 2 * width)
    for part, (ours, theirs) in enumerate(
        ((second, first), (everything, everything), (first, second))
    ):
        for q, (r, h) in enumerate(quarters):
            mask = (i + r * half < size) & (j + h * half < size)
            x = dot(tt[hs[r], ours], xx[theirs, hs[h]])
            lsend[part, q] = jnp.where(mask, x, 0.0).astype(BF16)

        @pl.when(sends[0])
        def _():
            env_copy(0, part).start()

        for q, (r, h) in enumerate(quarters):
            mask = (i + r * half < size) & (j + h * half < size)
            x = dot_nt(yy[hs[r], theirs], ff[hs[h], ours])
            rsend[part, q] = jnp.where(mask, x, 0.0).astype(BF16)

        @pl.when(sends[1])
        def _():
            env_copy(1, part).start()

    first_half(par, f, corr, weight, cross)
    a, scale, energy = coefficients(par, None, energy)
    ratio[...] = jnp.broadcast_to(jnp.where(lane == 0, a, scale), (8, 128))
    for which in (0, 1):

        @pl.when(sends[which])
        def _():
            ratio_copy(which).start()

    energy_o[...] = jnp.broadcast_to(energy, (8, 128))
    for h in (0, 1):

        def step(i, _):
            rows = pl.ds(pl.multiple_of(i * ROWS, ROWS), ROWS)
            v = a * vec[h, rows] + scale * cb[h, rows].astype(F32)
            ground_o[rows, hs[h]] = v * (width * math.sqrt(n))
            return 0

        lax.fori_loop(0, width // ROWS, step, 0)

    handoff = n * width * math.sqrt(width)

    def combine(which, got, out):
        env_copy(which, None).wait_recv()
        ratio_copy(which).wait_recv()
        row = ratio_in[which, 0:1]
        a = jnp.sum(jnp.where(lane == 0, row, 0.0), axis=1, keepdims=True)
        b = jnp.sum(jnp.where(lane == 1, row, 0.0), axis=1, keepdims=True)
        weights = (handoff * a * a, handoff * a * b, handoff * b * b)
        for q, (r, h) in enumerate(quarters):
            x = sum(weights[part] * got[part, q].astype(F32) for part in range(3))
            out[hs[r], hs[h]] = x.astype(BF16)
            if r != h:
                out[hs[h], hs[r]] = x.T.astype(BF16)

    @pl.when(seg > 0)
    def _():
        combine(0, lrecv, lenv_o)

    @pl.when(seg < nseg - 1)
    def _():
        combine(1, rrecv, renv_o)

    x_whole(0, f).wait_send()
    c_copy(0, 1 - f).wait_send()
    for which in (0, 1):

        @pl.when(sends[which])
        def _():
            env_copy(which, None).wait_send()
            ratio_copy(which).wait_send()

    @pl.when(seg == 0)
    def _():
        own_left.wait()

    @pl.when(seg == nseg - 1)
    def _():
        own_right.wait()


def store(ground, energy, lenv, renv, ground_o, energy_o, lenv_o, renv_o, sem):
    copies = [
        pltpu.make_async_copy(src, dst.at[0, 0], sem.at[i])
        for i, (src, dst) in enumerate(((ground, ground_o), (lenv, lenv_o), (renv, renv_o)))
    ]
    for copy in copies:
        copy.start()
    energy_o[0] = energy[0, 0]
    for copy in copies:
        copy.wait()


def per_device(
    guess_blocks, onsite_left, onsite_right, hopping_left, hopping_right, sector_dims, kept_dims
):
    n, nseg = lax.axis_size("blk"), lax.axis_size("seg")
    width = guess_blocks.shape[-1]
    half = width // 2
    square, halves = (width, width), (2, width, half)
    forms = (3, 3, half, half)
    hbm = pl.BlockSpec(memory_space=pltpu.HBM)
    vmem = pl.BlockSpec(memory_space=pltpu.VMEM)
    any_space = pl.BlockSpec(memory_space=pl.ANY)
    smem = pl.BlockSpec(memory_space=pltpu.SMEM)
    dma = pltpu.SemaphoreType.DMA
    scratch = [
        pltpu.VMEM((2,) + square, BF16),
        pltpu.VMEM((2 * width, width), BF16),
        pltpu.VMEM(square, BF16),
        pltpu.VMEM(square, BF16),
        pltpu.VMEM(halves, BF16),
        pltpu.VMEM(square, BF16),
        pltpu.VMEM(halves, F32),
        pltpu.VMEM(halves, F32),
        pltpu.VMEM(halves, F32),
        pltpu.VMEM(halves, F32),
        pltpu.VMEM(halves, BF16),
        pltpu.VMEM((2,) + halves, BF16),
        pltpu.VMEM(halves, BF16),
        pltpu.VMEM((2,) + halves, BF16),
        pltpu.VMEM((width, 2 * width), BF16),
        pltpu.VMEM(square, BF16),
        pltpu.VMEM((width, half), BF16),
        pltpu.VMEM((width, 2 * width), BF16),
        pltpu.VMEM((width, 2 * width), BF16),
        pltpu.VMEM((2 * width, width), BF16),
        pltpu.VMEM((width, 2 * width), BF16),
        pltpu.VMEM(forms, BF16),
        pltpu.VMEM(forms, BF16),
        pltpu.VMEM(forms, BF16),
        pltpu.VMEM(forms, BF16),
        pltpu.VMEM((8, 128), F32),
        pltpu.VMEM((2, 8, 128), F32),
        pltpu.VMEM((2, 8, 128), F32),
        pltpu.VMEM((2, n, 128), F32),
        pltpu.SMEM((1, 2), jnp.int32),
        pltpu.SMEM((1, 1), jnp.int32),
        dma((8,)), dma((2,)), dma((2, 2)), dma((2,)), dma((2, 2)), dma((2,)), dma((2,)),
        dma((3,)), dma((2,)), dma((2,)), dma((2,)), dma((2,)),
    ]
    results = pl.pallas_call(
        functools.partial(kernel, n, nseg, width),
        out_shape=(
            pltpu.VMEM(square, F32),
            pltpu.VMEM((8, 128), F32),
            pltpu.VMEM(square, BF16),
            pltpu.VMEM(square, BF16),
        ),
        in_specs=[hbm] * 7,
        out_specs=(vmem,) * 4,
        scratch_shapes=scratch,
        compiler_params=pltpu.CompilerParams(
            collective_id=0, has_side_effects=True, vmem_limit_bytes=58 * 2**20
        ),
    )(
        guess_blocks[0, 0],
        onsite_left[0, 0],
        onsite_right[0, 0].reshape(2 * width, width),
        hopping_left[0, 0],
        hopping_right[0, 0],
        sector_dims[0],
        kept_dims,
    )
    return pl.pallas_call(
        store,
        out_shape=(
            jax.ShapeDtypeStruct((1, 1) + square, F32),
            jax.ShapeDtypeStruct((1,), F32),
            jax.ShapeDtypeStruct((1, 1) + square, BF16),
            jax.ShapeDtypeStruct((1, 1) + square, BF16),
        ),
        in_specs=[vmem] * 4,
        out_specs=(any_space, smem, any_space, any_space),
        scratch_shapes=[dma((3,))],
        compiler_params=pltpu.CompilerParams(vmem_limit_bytes=2**20),
    )(*results)


def solution(mesh):
    in_specs = (
        P("seg", "blk", None, None),
        P("seg", "blk", None, None, None),
        P("seg", "blk", None, None, None),
        P("seg", "blk", None, None),
        P("seg", "blk", None, None),
        P("seg", "blk", None),
        P("seg", "blk"),
    )
    out_specs = (
        P("seg", "blk", None, None),
        P("seg"),
        P("seg", "blk", None, None),
        P("seg", "blk", None, None),
    )
    return jax.shard_map(
        per_device, mesh=mesh, in_specs=in_specs, out_specs=out_specs, check_vma=False
    )
```

```python
import functools
import math

import jax
import jax.numpy as jnp
from jax import lax
from jax.experimental import pallas as pl
from jax.experimental.pallas import tpu as pltpu
from jax.sharding import PartitionSpec as P

ITERS = 4
MESH = pl.DeviceIdType.MESH
F32 = jnp.float32
BF16 = jnp.bfloat16
SIDE = 4
ROWS = 32
OUTSIDE = 3e38


def dot(a, b):
    return lax.dot_general(a, b, (((1,), (0,)), ((), ())), preferred_element_type=F32)


def dot_nt(a, b):
    return lax.dot_general(a, b, (((1,), (1,)), ((), ())), preferred_element_type=F32)


def fold(x):
    rows, cols = x.shape
    return jnp.sum(x.reshape(rows // 8, 8, cols), axis=0)


def total(x):
    return jnp.sum(jnp.sum(x, axis=0, keepdims=True), axis=1, keepdims=True)


def kernel(
    n, nseg, width,
    guess_h, left_h, right_h, hopl_h, hopr_h, dims_h, kept_h,
    ground_o, energy_o, lrecv, rrecv, ratio_in,
    lv, rv, hl, hlt, hrc, gv, diag, vec, img, acc, cb, xr, cs, cr, pp, rm, qq,
    ff, tt, xx, yy, lsend, rsend, ratio, arsrc, arbuf, dims, kept,
    load_sem, xs_sem, xr_sem, cs_sem, cr_sem, as_sem, ar_sem, env_s, env_r,
    ratio_s, ratio_r, ready,
):
    me = lax.axis_index("blk")
    seg = lax.axis_index("seg")
    right, left = lax.rem(me + 1, n), lax.rem(me + n - 1, n)
    half = width // 2
    hs = (pl.ds(0, half), pl.ds(half, half))
    steps = half // ROWS

    loads = [
        pltpu.make_async_copy(src, dst, load_sem.at[i])
        for i, (src, dst) in enumerate(
            (
                (dims_h, dims),
                (guess_h, gv),
                (hopl_h, hl),
                (hopr_h.at[:, hs[0]], hrc.at[0]),
                (hopr_h.at[:, hs[1]], hrc.at[1]),
                (left_h, lv),
                (right_h, rv),
                (kept_h, kept),
            )
        )
    ]
    for copy in loads:
        copy.start()

    y, z = lax.rem(me, SIDE), me // SIDE
    layers = n // SIDE
    above = lax.rem(z + 1, layers) * SIDE + y
    below = lax.rem(z + layers - 1, layers) * SIDE + y
    barrier = pltpu.get_barrier_semaphore()

    def greet(**device):
        pl.semaphore_signal(barrier, inc=1, device_id=device, device_id_type=MESH)

    for d in range(1, SIDE):
        greet(blk=z * SIDE + lax.rem(y + d, SIDE))
    greet(blk=above)
    greet(blk=below)
    for d in (1, nseg - 1):
        greet(seg=lax.rem(seg + d, nseg))

    @pl.when(y == SIDE - 1)
    def _():
        greet(blk=right)

    @pl.when(y == 0)
    def _():
        greet(blk=left)

    ends = jnp.where(y == SIDE - 1, 1, 0) + jnp.where(y == 0, 1, 0)

    def everyone():
        for _ in range(layers // 2):
            for which, other in ((0, above), (1, below)):
                pl.semaphore_signal(
                    ready.at[which], inc=1, device_id={"blk": other}, device_id_type=MESH
                )
            for which in (0, 1):
                pl.semaphore_wait(ready.at[which], 1)

    loads[0].wait()
    live_rows, live_cols = dims[0, 0], dims[0, 1]

    def live(row0, h, rows):
        i = lax.broadcasted_iota(jnp.int32, (rows, half), 0) + row0
        j = lax.broadcasted_iota(jnp.int32, (rows, half), 1) + h * half
        return (i < live_rows) & (j < live_cols)

    def x_copy(par, h, rc):
        rows = pl.ds(rc * half, half)
        return pltpu.make_async_remote_copy(
            src_ref=cb.at[h, rows], dst_ref=xr.at[par, h, rows],
            send_sem=xs_sem.at[h], recv_sem=xr_sem.at[par, h],
            device_id={"blk": left}, device_id_type=MESH,
        )

    def x_whole(par, h):
        return pltpu.make_async_remote_copy(
            src_ref=cb.at[h], dst_ref=xr.at[par, h],
            send_sem=xs_sem.at[h], recv_sem=xr_sem.at[par, h],
            device_id={"blk": left}, device_id_type=MESH,
        )

    def c_copy(par, h):
        return pltpu.make_async_remote_copy(
            src_ref=cs.at[h], dst_ref=cr.at[par, h],
            send_sem=cs_sem.at[h], recv_sem=cr_sem.at[par, h],
            device_id={"blk": right}, device_id_type=MESH,
        )

    loads[1].wait()

    for h in (0, 1):

        def step(i, _):
            row0 = pl.multiple_of(i * ROWS, ROWS)
            rows = pl.ds(row0, ROWS)
            cb[h, rows] = jnp.where(live(row0, h, ROWS), gv[rows, hs[h]], jnp.zeros((), BF16))
            return 0

        lax.fori_loop(0, width // ROWS, step, 0)

    pl.semaphore_wait(barrier, SIDE - 1 + 4 + ends)
    for h in (0, 1):
        for rc in (0, 1):
            x_copy(0, h, rc).start()

    loads[2].wait()

    @pl.when(me == n - 1)
    def _():
        hl[...] = jnp.zeros_like(hl)

    hlt[...] = hl[...].T
    loads[3].wait()
    loads[4].wait()

    def couple(par, halves):
        for h in (0, 1):
            rm[:, hs[h]] = dot(hlt[...], cb[h]).astype(BF16)
        for h in halves:
            cs[h] = dot(rm[...], hrc[h]).astype(BF16)
            c_copy(par, h).start()

    def products(k):
        for h in (0, 1):
            pp[:, pl.ds(k * width + h * half, half)] = dot(lv[k], cb[h]).astype(BF16)

    def onsite():
        for h in (0, 1):
            acc[h] = dot(pp[...], rv[:, hs[h]])

    def ar_whole(par):
        return pltpu.make_async_remote_copy(
            src_ref=arbuf.at[par, pl.ds(0, n - 1)], dst_ref=arbuf.at[par, pl.ds(0, n - 1)],
            send_sem=as_sem.at[par], recv_sem=ar_sem.at[par],
            device_id={"blk": right}, device_id_type=MESH,
        )

    lane = lax.broadcasted_iota(jnp.int32, (1, 128), 1)

    def field_sums():
        sums = (jnp.zeros((8, half), F32),) * 3
        for h in (0, 1):

            def step(i, sums):
                corr, weight, cross = sums
                rows = pl.ds(pl.multiple_of(i * ROWS, ROWS), ROWS)
                c = cb[h, rows].astype(F32)
                return (
                    corr + fold(vec[h, rows] * c),
                    weight + fold(c * c),
                    cross + fold(img[h, rows] * c),
                )

            sums = lax.fori_loop(0, width // ROWS, step, sums)
        row = jnp.zeros((1, 128), F32)
        for k in range(3):
            row = jnp.where(lane == k, total(sums[k]), row)
        return row

    def first_half(par, f, row):
        x_whole(par, f).wait_recv()
        qq[...] = dot(hl[...], xr[par, f]).astype(BF16)
        curv = jnp.zeros((8, half), F32)
        for h in (0, 1):
            part = dot_nt(qq[...], hrc[f, hs[h]])
            local = acc[h]
            curv = curv + fold(cb[h].astype(F32) * (local + 2.0 * part))
            acc[h] = local + part
        c_copy(par, 1 - f).wait_recv()
        curv = curv + 2.0 * fold(cb[1 - f].astype(F32) * cr[par, 1 - f].astype(F32))
        row = jnp.where(lane == 3, total(curv), row)
        arsrc[par, 0:1] = row
        arbuf[par, n - 1 : n] = row
        for d in range(1, n):
            pltpu.make_async_remote_copy(
                src_ref=arsrc.at[par, pl.ds(0, 1)], dst_ref=arbuf.at[par, pl.ds(d - 1, 1)],
                send_sem=as_sem.at[par], recv_sem=ar_sem.at[par],
                device_id={"blk": lax.rem(me + d, n)}, device_id_type=MESH,
            ).start()

    def second_half(par, f):
        x_whole(par, 1 - f).wait_recv()
        qq[...] = dot(hl[...], xr[par, 1 - f]).astype(BF16)
        for h in (0, 1):
            acc[h] = acc[h] + dot_nt(qq[...], hrc[1 - f, hs[h]])

    def coefficients(par, start, energy):
        whole = ar_whole(par)
        whole.wait_recv()
        tot = jnp.sum(arbuf[par], axis=0, keepdims=True)
        corr, weight, cross, curv = (
            jnp.sum(jnp.where(lane == k, tot, 0.0), axis=1, keepdims=True) for k in range(4)
        )
        whole.wait_send()
        span = weight - corr * corr
        length = jnp.sqrt(span)
        off = (cross - corr * energy) / length
        lower = (curv - 2.0 * corr * cross + corr * corr * energy) / span
        gap = (energy - lower) / 2.0
        radius = jnp.sqrt(gap * gap + off * off)
        keep = radius - gap
        turn = -off
        norm = jnp.sqrt(keep * keep + turn * turn)
        scale = turn / (length * norm)
        a = keep / norm - scale * corr
        new = (energy + lower) / 2.0 - radius
        if start is None:
            return a, scale, new
        a = jnp.where(start, 0.0, a)
        scale = jnp.where(start, 1.0 / length, scale)
        new = jnp.where(start, lower, new)
        return a, scale, new

    def prepare():
        vec[...] = jnp.zeros_like(vec)
        img[...] = jnp.zeros_like(img)
        i = lax.broadcasted_iota(jnp.int32, (128, 128), 0)
        eye = i == lax.broadcasted_iota(jnp.int32, (128, 128), 1)
        for h in (0, 1):
            cols = [
                [
                    jnp.sum(
                        jnp.where(
                            eye,
                            rv[pl.ds(k * width + b, 128), pl.ds(b, 128)].astype(F32),
                            0.0,
                        ),
                        axis=0,
                        keepdims=True,
                    )
                    for b in range(h * half, (h + 1) * half, 128)
                ]
                for k in (0, 1)
            ]
            cols = [jnp.concatenate(c, axis=1) for c in cols]
            for b in range(0, width, 128):
                value = jnp.zeros((128, half), F32)
                for k in (0, 1):
                    block = lv[k, pl.ds(b, 128), pl.ds(b, 128)].astype(F32)
                    col = jnp.sum(jnp.where(eye, block, 0.0), axis=1, keepdims=True)
                    value = value + col * cols[k]
                diag[h, pl.ds(b, 128)] = jnp.where(live(b, h, 128), value, OUTSIDE)

    def update(par, f, last, a, scale, energy):
        for h in (1 - f, f):
            if h is f:
                c_copy(par, f).wait_recv()

            def chunk(rc, _, h=h):
                def step(i, _):
                    rows = pl.ds(pl.multiple_of(rc * half + i * ROWS, ROWS), ROWS)
                    c = cb[h, rows].astype(F32)
                    v = a * vec[h, rows] + scale * c
                    m = a * img[h, rows] + scale * (acc[h, rows] + cr[par, h, rows].astype(F32))
                    vec[h, rows] = v
                    img[h, rows] = m
                    inv = pl.reciprocal(1.0 + jnp.abs(diag[h, rows] - energy), approx=True)
                    cb[h, rows] = ((m - energy * v) * inv).astype(BF16)
                    return 0

                lax.fori_loop(0, steps, step, 0)
                if h is not f:
                    x_copy(1 - par, h, rc).start()
                else:

                    @pl.when(jnp.logical_not(last))
                    def _():
                        x_copy(1 - par, h, rc).start()

                return 0

            lax.fori_loop(0, 2, chunk, 0)

    couple(0, (1, 0))
    loads[5].wait()
    loads[6].wait()
    prepare()

    def iteration(t, energy):
        par = lax.rem(t, 2)
        f = par

        @pl.when(t > 0)
        def _():
            for h in (0, 1):
                c_copy(0, h).wait_send()
            couple(par, (1 - f, f))

        products(0)
        products(1)
        onsite()
        row = field_sums()

        @pl.when(t == 0)
        def _():
            everyone()

        first_half(par, f, row)
        second_half(par, f)
        a, scale, energy = coefficients(par, t == 0, energy)
        for h in (0, 1):
            x_whole(0, h).wait_send()
        update(par, f, t == ITERS - 1, a, scale, energy)
        return energy

    energy = lax.fori_loop(0, ITERS, iteration, jnp.zeros((1, 1), F32))
    par = ITERS % 2
    f = par
    for h in (0, 1):
        c_copy(0, h).wait_send()
    couple(par, (1 - f,))
    products(0)

    loads[7].wait()
    size = kept[0, 0]
    blocks = [(r, h) for r in range(width // 128) for h in range(r + 1)]

    def env_copy(which, part):
        src, dst = ((lsend, lrecv), (rsend, rrecv))[which]
        other = lax.rem(seg + (1, nseg - 1)[which], nseg)
        if part is not None:
            src, dst = src.at[part], dst.at[part]
        return pltpu.make_async_remote_copy(
            src_ref=src, dst_ref=dst, send_sem=env_s.at[which], recv_sem=env_r.at[which],
            device_id={"seg": other}, device_id_type=MESH,
        )

    def ratio_copy(which):
        other = lax.rem(seg + (1, nseg - 1)[which], nseg)
        return pltpu.make_async_remote_copy(
            src_ref=ratio.at[pl.ds(0, 1)], dst_ref=ratio_in.at[which, pl.ds(0, 1)],
            send_sem=ratio_s.at[which], recv_sem=ratio_r.at[which],
            device_id={"seg": other}, device_id_type=MESH,
        )

    sends = (seg < nseg - 1, seg > 0)
    i = lax.broadcasted_iota(jnp.int32, (half, half), 0)
    j = lax.broadcasted_iota(jnp.int32, (half, half), 1)

    def put(send, part, r, h, x):
        x = jnp.where((i + r * half < size) & (j + h * half < size), x, 0.0).astype(BF16)
        for q, (row, col) in enumerate(blocks):
            if row // 2 == r and col // 2 == h:
                b, c = row % 2 * 128, col % 2 * 128
                send[part, q] = x[b : b + 128, c : c + 128]

    quarters = ((0, 0), (1, 0), (1, 1))
    first, second = pl.ds(0, width), pl.ds(width, width)
    for h in (0, 1):
        ff[:, hs[h]] = cb[h]
        ff[:, pl.ds(width + h * half, half)] = vec[h].astype(BF16)
    tt[:, first] = ff[:, first].T
    tt[:, second] = ff[:, second].T
    for h in (0, 1):
        xx[first, hs[h]] = dot(lv[0], ff[:, pl.ds(width + h * half, half)]).astype(BF16)
        yy[:, hs[h]] = dot(ff[:, second], rv[first, hs[h]]).astype(BF16)
    xx[second, :] = pp[:, first]
    for h in (0, 1):
        yy[:, pl.ds(width + h * half, half)] = dot(ff[:, first], rv[first, hs[h]]).astype(BF16)
    everything = pl.ds(0, 2 * width)
    for part, (ours, theirs) in enumerate(
        ((second, first), (everything, everything), (first, second))
    ):
        for r, h in quarters:
            put(lsend, part, r, h, dot(tt[hs[r], ours], xx[theirs, hs[h]]))

        @pl.when(sends[0])
        def _():
            env_copy(0, part).start()

        for r, h in quarters:
            put(rsend, part, r, h, dot_nt(yy[hs[r], theirs], ff[hs[h], ours]))

        @pl.when(sends[1])
        def _():
            env_copy(1, part).start()

    products(1)
    onsite()
    row = field_sums()
    first_half(par, f, row)
    a, scale, energy = coefficients(par, None, energy)
    ratio[...] = jnp.broadcast_to(jnp.where(lane == 0, a, scale), (8, 128))
    for which in (0, 1):

        @pl.when(sends[which])
        def _():
            ratio_copy(which).start()

    energy_o[...] = jnp.broadcast_to(energy, (8, 128))
    for h in (0, 1):

        def step(i, _):
            rows = pl.ds(pl.multiple_of(i * ROWS, ROWS), ROWS)
            v = a * vec[h, rows] + scale * cb[h, rows].astype(F32)
            ground_o[rows, hs[h]] = v * (width * math.sqrt(n))
            return 0

        lax.fori_loop(0, width // ROWS, step, 0)

    for which, receives in ((0, seg > 0), (1, seg < nseg - 1)):

        @pl.when(receives)
        def _():
            env_copy(which, None).wait_recv()
            ratio_copy(which).wait_recv()

    x_whole(0, f).wait_send()
    c_copy(0, 1 - f).wait_send()
    for which in (0, 1):

        @pl.when(sends[which])
        def _():
            env_copy(which, None).wait_send()
            ratio_copy(which).wait_send()


def store(
    n, nseg, width,
    ground, energy, lrecv, rrecv, ratio_in, left_h, right_h,
    ground_o, energy_o, lenv_o, renv_o, lb, rb, sem,
):
    seg = lax.axis_index("seg")
    out = pltpu.make_async_copy(ground, ground_o.at[0, 0], sem.at[0])
    out.start()
    energy_o[0] = energy[0, 0]
    handoff = n * width * math.sqrt(width)
    lane = lax.broadcasted_iota(jnp.int32, (1, 128), 1)
    blocks = [(r, h) for r in range(width // 128) for h in range(r + 1)]
    sides = (
        (seg == 0, left_h.at[0], lrecv, lb, lenv_o),
        (seg == nseg - 1, right_h.at[pl.ds(0, width)], rrecv, rb, renv_o),
    )
    for which, (edge, own, got, made, dst) in enumerate(sides):

        @pl.when(edge)
        def _():
            pltpu.make_async_copy(own, dst.at[0, 0], sem.at[1 + which]).start()

        @pl.when(jnp.logical_not(edge))
        def _():
            row = ratio_in[which, 0:1]
            a = jnp.sum(jnp.where(lane == 0, row, 0.0), axis=1, keepdims=True)
            b = jnp.sum(jnp.where(lane == 1, row, 0.0), axis=1, keepdims=True)
            weights = (handoff * a * a, handoff * a * b, handoff * b * b)
            for q, (r, h) in enumerate(blocks):
                x = sum(weights[part] * got[part, q].astype(F32) for part in range(3))
                rows, cols = pl.ds(r * 128, 128), pl.ds(h * 128, 128)
                made[rows, cols] = x.astype(BF16)
                if r != h:
                    made[cols, rows] = x.T.astype(BF16)
            pltpu.make_async_copy(made, dst.at[0, 0], sem.at[1 + which]).start()

    out.wait()
    for which, (edge, own, got, made, dst) in enumerate(sides):
        pltpu.make_async_copy(made, dst.at[0, 0], sem.at[1 + which]).wait()


def per_device(
    guess_blocks, onsite_left, onsite_right, hopping_left, hopping_right, sector_dims, kept_dims
):
    n, nseg = lax.axis_size("blk"), lax.axis_size("seg")
    width = guess_blocks.shape[-1]
    half = width // 2
    square, halves = (width, width), (2, width, half)
    count = (width // 128) * (width // 128 + 1) // 2
    forms = (3, count, 128, 128)
    hbm = pl.BlockSpec(memory_space=pltpu.HBM)
    vmem = pl.BlockSpec(memory_space=pltpu.VMEM)
    any_space = pl.BlockSpec(memory_space=pl.ANY)
    smem = pl.BlockSpec(memory_space=pltpu.SMEM)
    dma = pltpu.SemaphoreType.DMA
    scratch = [
        pltpu.VMEM((2,) + square, BF16),
        pltpu.VMEM((2 * width, width), BF16),
        pltpu.VMEM(square, BF16),
        pltpu.VMEM(square, BF16),
        pltpu.VMEM(halves, BF16),
        pltpu.VMEM(square, BF16),
        pltpu.VMEM(halves, F32),
        pltpu.VMEM(halves, F32),
        pltpu.VMEM(halves, F32),
        pltpu.VMEM(halves, F32),
        pltpu.VMEM(halves, BF16),
        pltpu.VMEM((2,) + halves, BF16),
        pltpu.VMEM(halves, BF16),
        pltpu.VMEM((2,) + halves, BF16),
        pltpu.VMEM((width, 2 * width), BF16),
        pltpu.VMEM(square, BF16),
        pltpu.VMEM((width, half), BF16),
        pltpu.VMEM((width, 2 * width), BF16),
        pltpu.VMEM((width, 2 * width), BF16),
        pltpu.VMEM((2 * width, width), BF16),
        pltpu.VMEM((width, 2 * width), BF16),
        pltpu.VMEM(forms, BF16),
        pltpu.VMEM(forms, BF16),
        pltpu.VMEM((8, 128), F32),
        pltpu.VMEM((2, 8, 128), F32),
        pltpu.VMEM((2, n, 128), F32),
        pltpu.SMEM((1, 2), jnp.int32),
        pltpu.SMEM((1, 1), jnp.int32),
        dma((8,)), dma((2,)), dma((2, 2)), dma((2,)), dma((2, 2)), dma((2,)), dma((2,)),
        dma((2,)), dma((2,)), dma((2,)), dma((2,)),
        pltpu.SemaphoreType.REGULAR((2,)),
    ]
    left, right = onsite_left[0, 0], onsite_right[0, 0].reshape(2 * width, width)
    results = pl.pallas_call(
        functools.partial(kernel, n, nseg, width),
        out_shape=(
            pltpu.VMEM(square, F32),
            pltpu.VMEM((8, 128), F32),
            pltpu.VMEM(forms, BF16),
            pltpu.VMEM(forms, BF16),
            pltpu.VMEM((2, 8, 128), F32),
        ),
        in_specs=[hbm] * 7,
        out_specs=(vmem,) * 5,
        scratch_shapes=scratch,
        compiler_params=pltpu.CompilerParams(
            collective_id=0, has_side_effects=True, vmem_limit_bytes=58 * 2**20
        ),
    )(
        guess_blocks[0, 0],
        left,
        right,
        hopping_left[0, 0],
        hopping_right[0, 0],
        sector_dims[0],
        kept_dims,
    )
    return pl.pallas_call(
        functools.partial(store, n, nseg, width),
        out_shape=(
            jax.ShapeDtypeStruct((1, 1) + square, F32),
            jax.ShapeDtypeStruct((1,), F32),
            jax.ShapeDtypeStruct((1, 1) + square, BF16),
            jax.ShapeDtypeStruct((1, 1) + square, BF16),
        ),
        in_specs=[vmem] * 5 + [any_space] * 2,
        out_specs=(any_space, smem, any_space, any_space),
        scratch_shapes=[pltpu.VMEM(square, BF16), pltpu.VMEM(square, BF16), dma((3,))],
        compiler_params=pltpu.CompilerParams(vmem_limit_bytes=4 * 2**20),
    )(*results, left, right)


def solution(mesh):
    in_specs = (
        P("seg", "blk", None, None),
        P("seg", "blk", None, None, None),
        P("seg", "blk", None, None, None),
        P("seg", "blk", None, None),
        P("seg", "blk", None, None),
        P("seg", "blk", None),
        P("seg", "blk"),
    )
    out_specs = (
        P("seg", "blk", None, None),
        P("seg"),
        P("seg", "blk", None, None),
        P("seg", "blk", None, None),
    )
    return jax.shard_map(
        per_device, mesh=mesh, in_specs=in_specs, out_specs=out_specs, check_vma=False
    )
```

```python
import functools
import math

import jax
import jax.numpy as jnp
from jax import lax
from jax.experimental import pallas as pl
from jax.experimental.pallas import tpu as pltpu
from jax.sharding import PartitionSpec as P

ITERS = 4
MESH = pl.DeviceIdType.MESH
F32 = jnp.float32
BF16 = jnp.bfloat16
SIDE = 4
TILE = 256
ROWS = 32
OUTSIDE = 3e38


def dot(a, b):
    return lax.dot_general(a, b, (((1,), (0,)), ((), ())), preferred_element_type=F32)


def dot_nt(a, b):
    return lax.dot_general(a, b, (((1,), (1,)), ((), ())), preferred_element_type=F32)


def fold(x):
    rows, cols = x.shape
    return jnp.sum(x.reshape(rows // 8, 8, cols), axis=0)


def total(x):
    return jnp.sum(jnp.sum(x, axis=0, keepdims=True), axis=1, keepdims=True)


def kernel(
    n, nseg, width,
    guess_h, left_h, right_h, hopl_h, hopr_h, dims_h, kept_h,
    ground_o, energy_o, lrecv, rrecv, ratio_in,
    lv, rv, hl, hlt, hrc, gv, diag, vec, img, acc, cb, xr, cs, cr, pp, rm, qq,
    ff, tt, xx, yy, lsend, rsend, ratio, arsrc, arbuf, dims, kept,
    load_sem, xs_sem, xr_sem, cs_sem, cr_sem, as_sem, ar_sem, env_s, env_r,
    ratio_s, ratio_r, ready,
):
    me = lax.axis_index("blk")
    seg = lax.axis_index("seg")
    right, left = lax.rem(me + 1, n), lax.rem(me + n - 1, n)
    half = width // 2
    hs = (pl.ds(0, half), pl.ds(half, half))
    steps = half // ROWS

    loads = [
        pltpu.make_async_copy(src, dst, load_sem.at[i])
        for i, (src, dst) in enumerate(
            (
                (dims_h, dims),
                (guess_h, gv),
                (hopl_h, hl),
                (hopr_h.at[:, hs[0]], hrc.at[0]),
                (hopr_h.at[:, hs[1]], hrc.at[1]),
                (left_h, lv),
                (right_h, rv),
                (kept_h, kept),
            )
        )
    ]
    for copy in loads:
        copy.start()

    y, z = lax.rem(me, SIDE), me // SIDE
    layers = n // SIDE
    above = lax.rem(z + 1, layers) * SIDE + y
    below = lax.rem(z + layers - 1, layers) * SIDE + y
    barrier = pltpu.get_barrier_semaphore()

    def greet(**device):
        pl.semaphore_signal(barrier, inc=1, device_id=device, device_id_type=MESH)

    for d in range(1, SIDE):
        greet(blk=z * SIDE + lax.rem(y + d, SIDE))
    greet(blk=above)
    greet(blk=below)
    for d in (1, nseg - 1):
        greet(seg=lax.rem(seg + d, nseg))

    @pl.when(y == SIDE - 1)
    def _():
        greet(blk=right)

    @pl.when(y == 0)
    def _():
        greet(blk=left)

    ends = jnp.where(y == SIDE - 1, 1, 0) + jnp.where(y == 0, 1, 0)

    def everyone():
        for _ in range(layers // 2):
            for which, other in ((0, above), (1, below)):
                pl.semaphore_signal(
                    ready.at[which], inc=1, device_id={"blk": other}, device_id_type=MESH
                )
            for which in (0, 1):
                pl.semaphore_wait(ready.at[which], 1)

    loads[0].wait()
    live_rows, live_cols = dims[0, 0], dims[0, 1]

    def live(row0, h, rows):
        i = lax.broadcasted_iota(jnp.int32, (rows, half), 0) + row0
        j = lax.broadcasted_iota(jnp.int32, (rows, half), 1) + h * half
        return (i < live_rows) & (j < live_cols)

    def x_copy(par, h, rc):
        rows = pl.ds(rc * half, half)
        return pltpu.make_async_remote_copy(
            src_ref=cb.at[h, rows], dst_ref=xr.at[par, h, rows],
            send_sem=xs_sem.at[h], recv_sem=xr_sem.at[par, h],
            device_id={"blk": left}, device_id_type=MESH,
        )

    def x_whole(par, h):
        return pltpu.make_async_remote_copy(
            src_ref=cb.at[h], dst_ref=xr.at[par, h],
            send_sem=xs_sem.at[h], recv_sem=xr_sem.at[par, h],
            device_id={"blk": left}, device_id_type=MESH,
        )

    def c_copy(par, h):
        return pltpu.make_async_remote_copy(
            src_ref=cs.at[h], dst_ref=cr.at[par, h],
            send_sem=cs_sem.at[h], recv_sem=cr_sem.at[par, h],
            device_id={"blk": right}, device_id_type=MESH,
        )

    loads[1].wait()

    for h in (0, 1):

        def step(i, _):
            row0 = pl.multiple_of(i * ROWS, ROWS)
            rows = pl.ds(row0, ROWS)
            cb[h, rows] = jnp.where(live(row0, h, ROWS), gv[rows, hs[h]], jnp.zeros((), BF16))
            return 0

        lax.fori_loop(0, width // ROWS, step, 0)

    pl.semaphore_wait(barrier, SIDE - 1 + 4 + ends)
    for h in (0, 1):
        for rc in (0, 1):
            x_copy(0, h, rc).start()

    loads[2].wait()

    @pl.when(me == n - 1)
    def _():
        hl[...] = jnp.zeros_like(hl)

    hlt[...] = hl[...].T
    loads[3].wait()
    loads[4].wait()

    def c_tile(par, h, tile):
        rows = pl.ds(tile * TILE, TILE)
        return pltpu.make_async_remote_copy(
            src_ref=cs.at[h, rows], dst_ref=cr.at[par, h, rows],
            send_sem=cs_sem.at[h], recv_sem=cr_sem.at[par, h],
            device_id={"blk": right}, device_id_type=MESH,
        )

    def couple(par, halves):
        first = halves[0]
        for tile in range(width // TILE):
            rows = pl.ds(tile * TILE, TILE)
            for h in (0, 1):
                rm[rows, hs[h]] = dot(hlt[rows, :], cb[h]).astype(BF16)
            cs[first, rows] = dot(rm[rows, :], hrc[first]).astype(BF16)
            c_tile(par, first, tile).start()
        for h in halves[1:]:
            cs[h] = dot(rm[...], hrc[h]).astype(BF16)
            c_copy(par, h).start()

    def products(k):
        for h in (0, 1):
            pp[:, pl.ds(k * width + h * half, half)] = dot(lv[k], cb[h]).astype(BF16)

    def onsite():
        for h in (0, 1):
            acc[h] = dot(pp[...], rv[:, hs[h]])

    def ar_whole(par):
        return pltpu.make_async_remote_copy(
            src_ref=arbuf.at[par, pl.ds(0, n - 1)], dst_ref=arbuf.at[par, pl.ds(0, n - 1)],
            send_sem=as_sem.at[par], recv_sem=ar_sem.at[par],
            device_id={"blk": right}, device_id_type=MESH,
        )

    lane = lax.broadcasted_iota(jnp.int32, (1, 128), 1)

    def field_sums():
        sums = (jnp.zeros((8, half), F32),) * 3
        for h in (0, 1):

            def step(i, sums):
                corr, weight, cross = sums
                rows = pl.ds(pl.multiple_of(i * ROWS, ROWS), ROWS)
                c = cb[h, rows].astype(F32)
                return (
                    corr + fold(vec[h, rows] * c),
                    weight + fold(c * c),
                    cross + fold(img[h, rows] * c),
                )

            sums = lax.fori_loop(0, width // ROWS, step, sums)
        row = jnp.zeros((1, 128), F32)
        for k in range(3):
            row = jnp.where(lane == k, total(sums[k]), row)
        return row

    def first_half(par, f, row):
        x_whole(par, f).wait_recv()
        qq[...] = dot(hl[...], xr[par, f]).astype(BF16)
        curv = jnp.zeros((8, half), F32)
        for h in (0, 1):
            part = dot_nt(qq[...], hrc[f, hs[h]])
            local = acc[h]
            curv = curv + fold(cb[h].astype(F32) * (local + 2.0 * part))
            acc[h] = local + part
        c_copy(par, 1 - f).wait_recv()
        curv = curv + 2.0 * fold(cb[1 - f].astype(F32) * cr[par, 1 - f].astype(F32))
        row = jnp.where(lane == 3, total(curv), row)
        arsrc[par, 0:1] = row
        arbuf[par, n - 1 : n] = row
        for d in range(1, n):
            pltpu.make_async_remote_copy(
                src_ref=arsrc.at[par, pl.ds(0, 1)], dst_ref=arbuf.at[par, pl.ds(d - 1, 1)],
                send_sem=as_sem.at[par], recv_sem=ar_sem.at[par],
                device_id={"blk": lax.rem(me + d, n)}, device_id_type=MESH,
            ).start()

    def second_half(par, f):
        x_whole(par, 1 - f).wait_recv()
        qq[...] = dot(hl[...], xr[par, 1 - f]).astype(BF16)
        for h in (0, 1):
            acc[h] = acc[h] + dot_nt(qq[...], hrc[1 - f, hs[h]])

    def coefficients(par, start, energy):
        whole = ar_whole(par)
        whole.wait_recv()
        tot = jnp.sum(arbuf[par], axis=0, keepdims=True)
        corr, weight, cross, curv = (
            jnp.sum(jnp.where(lane == k, tot, 0.0), axis=1, keepdims=True) for k in range(4)
        )
        whole.wait_send()
        span = weight - corr * corr
        inverse = 1.0 / span
        slope = cross - corr * energy
        lower = (curv - 2.0 * corr * cross + corr * corr * energy) * inverse
        gap = (energy - lower) / 2.0
        square = slope * slope * inverse
        radius = jnp.sqrt(gap * gap + square)
        keep = radius - gap
        inorm = lax.rsqrt(keep * keep + square)
        scale = -slope * inverse * inorm
        a = keep * inorm - scale * corr
        new = (energy + lower) / 2.0 - radius
        if start is None:
            return a, scale, new
        a = jnp.where(start, 0.0, a)
        scale = jnp.where(start, lax.rsqrt(weight), scale)
        new = jnp.where(start, lower, new)
        return a, scale, new

    def prepare():
        vec[...] = jnp.zeros_like(vec)
        img[...] = jnp.zeros_like(img)
        i = lax.broadcasted_iota(jnp.int32, (128, 128), 0)
        eye = i == lax.broadcasted_iota(jnp.int32, (128, 128), 1)
        for h in (0, 1):
            cols = [
                [
                    jnp.sum(
                        jnp.where(
                            eye,
                            rv[pl.ds(k * width + b, 128), pl.ds(b, 128)].astype(F32),
                            0.0,
                        ),
                        axis=0,
                        keepdims=True,
                    )
                    for b in range(h * half, (h + 1) * half, 128)
                ]
                for k in (0, 1)
            ]
            cols = [jnp.concatenate(c, axis=1) for c in cols]
            for b in range(0, width, 128):
                value = jnp.zeros((128, half), F32)
                for k in (0, 1):
                    block = lv[k, pl.ds(b, 128), pl.ds(b, 128)].astype(F32)
                    col = jnp.sum(jnp.where(eye, block, 0.0), axis=1, keepdims=True)
                    value = value + col * cols[k]
                diag[h, pl.ds(b, 128)] = jnp.where(live(b, h, 128), value, OUTSIDE)

    def update(par, f, last, a, scale, energy):
        for h in (1 - f, f):
            if h is f:
                c_copy(par, f).wait_recv()

            def chunk(rc, _, h=h):
                def step(i, _):
                    rows = pl.ds(pl.multiple_of(rc * half + i * ROWS, ROWS), ROWS)
                    c = cb[h, rows].astype(F32)
                    v = a * vec[h, rows] + scale * c
                    m = a * img[h, rows] + scale * (acc[h, rows] + cr[par, h, rows].astype(F32))
                    vec[h, rows] = v
                    img[h, rows] = m
                    inv = pl.reciprocal(1.0 + jnp.abs(diag[h, rows] - energy), approx=True)
                    cb[h, rows] = ((m - energy * v) * inv).astype(BF16)
                    return 0

                lax.fori_loop(0, steps, step, 0)
                if h is not f:
                    x_copy(1 - par, h, rc).start()
                else:

                    @pl.when(jnp.logical_not(last))
                    def _():
                        x_copy(1 - par, h, rc).start()

                return 0

            lax.fori_loop(0, 2, chunk, 0)

    couple(0, (1, 0))
    loads[5].wait()
    loads[6].wait()
    prepare()

    def iteration(t, energy):
        par = lax.rem(t, 2)
        f = par

        @pl.when(t > 0)
        def _():
            for h in (0, 1):
                c_copy(0, h).wait_send()
            couple(par, (1 - f, f))

        products(0)
        products(1)
        onsite()
        row = field_sums()

        @pl.when(t == 0)
        def _():
            everyone()

        first_half(par, f, row)
        second_half(par, f)
        a, scale, energy = coefficients(par, t == 0, energy)
        for h in (0, 1):
            x_whole(0, h).wait_send()
        update(par, f, t == ITERS - 1, a, scale, energy)
        return energy

    energy = lax.fori_loop(0, ITERS, iteration, jnp.zeros((1, 1), F32))
    par = ITERS % 2
    f = par
    for h in (0, 1):
        c_copy(0, h).wait_send()
    couple(par, (1 - f,))
    products(0)

    loads[7].wait()
    size = kept[0, 0]
    blocks = [(r, h) for r in range(width // 128) for h in range(r + 1)]

    def env_copy(which, part):
        src, dst = ((lsend, lrecv), (rsend, rrecv))[which]
        other = lax.rem(seg + (1, nseg - 1)[which], nseg)
        if part is not None:
            src, dst = src.at[part], dst.at[part]
        return pltpu.make_async_remote_copy(
            src_ref=src, dst_ref=dst, send_sem=env_s.at[which], recv_sem=env_r.at[which],
            device_id={"seg": other}, device_id_type=MESH,
        )

    def ratio_copy(which):
        other = lax.rem(seg + (1, nseg - 1)[which], nseg)
        return pltpu.make_async_remote_copy(
            src_ref=ratio.at[pl.ds(0, 1)], dst_ref=ratio_in.at[which, pl.ds(0, 1)],
            send_sem=ratio_s.at[which], recv_sem=ratio_r.at[which],
            device_id={"seg": other}, device_id_type=MESH,
        )

    sends = (seg < nseg - 1, seg > 0)
    i = lax.broadcasted_iota(jnp.int32, (half, half), 0)
    j = lax.broadcasted_iota(jnp.int32, (half, half), 1)

    def put(send, part, r, h, x):
        x = jnp.where((i + r * half < size) & (j + h * half < size), x, 0.0).astype(BF16)
        for q, (row, col) in enumerate(blocks):
            if row // 2 == r and col // 2 == h:
                b, c = row % 2 * 128, col % 2 * 128
                send[part, q] = x[b : b + 128, c : c + 128]

    quarters = ((0, 0), (1, 0), (1, 1))
    first, second = pl.ds(0, width), pl.ds(width, width)
    for h in (0, 1):
        ff[:, hs[h]] = cb[h]
        ff[:, pl.ds(width + h * half, half)] = vec[h].astype(BF16)
    tt[:, first] = ff[:, first].T
    tt[:, second] = ff[:, second].T
    for h in (0, 1):
        xx[first, hs[h]] = dot(lv[0], ff[:, pl.ds(width + h * half, half)]).astype(BF16)
        yy[:, hs[h]] = dot(ff[:, second], rv[first, hs[h]]).astype(BF16)
    xx[second, :] = pp[:, first]
    for h in (0, 1):
        yy[:, pl.ds(width + h * half, half)] = dot(ff[:, first], rv[first, hs[h]]).astype(BF16)
    everything = pl.ds(0, 2 * width)
    def form(part):
        ours, theirs = ((second, first), (everything, everything), (first, second))[part]
        for r, h in quarters:
            put(lsend, part, r, h, dot(tt[hs[r], ours], xx[theirs, hs[h]]))

        @pl.when(sends[0])
        def _():
            env_copy(0, part).start()

        for r, h in quarters:
            put(rsend, part, r, h, dot_nt(yy[hs[r], theirs], ff[hs[h], ours]))

        @pl.when(sends[1])
        def _():
            env_copy(1, part).start()

    form(0)
    form(1)
    products(1)
    onsite()
    row = field_sums()
    first_half(par, f, row)
    form(2)
    a, scale, energy = coefficients(par, None, energy)
    ratio[...] = jnp.broadcast_to(jnp.where(lane == 0, a, scale), (8, 128))
    for which in (0, 1):

        @pl.when(sends[which])
        def _():
            ratio_copy(which).start()

    energy_o[...] = jnp.broadcast_to(energy, (8, 128))
    for h in (0, 1):

        def step(i, _):
            rows = pl.ds(pl.multiple_of(i * ROWS, ROWS), ROWS)
            v = a * vec[h, rows] + scale * cb[h, rows].astype(F32)
            ground_o[rows, hs[h]] = v * (width * math.sqrt(n))
            return 0

        lax.fori_loop(0, width // ROWS, step, 0)

    for which, receives in ((0, seg > 0), (1, seg < nseg - 1)):

        @pl.when(receives)
        def _():
            env_copy(which, None).wait_recv()
            ratio_copy(which).wait_recv()

    x_whole(0, f).wait_send()
    c_copy(0, 1 - f).wait_send()
    for which in (0, 1):

        @pl.when(sends[which])
        def _():
            env_copy(which, None).wait_send()
            ratio_copy(which).wait_send()


def store(
    n, nseg, width,
    ground, energy, lrecv, rrecv, ratio_in, left_h, right_h,
    ground_o, energy_o, lenv_o, renv_o, lb, rb, sem,
):
    seg = lax.axis_index("seg")
    out = pltpu.make_async_copy(ground, ground_o.at[0, 0], sem.at[0])
    out.start()
    energy_o[0] = energy[0, 0]
    handoff = n * width * math.sqrt(width)
    lane = lax.broadcasted_iota(jnp.int32, (1, 128), 1)
    blocks = [(r, h) for r in range(width // 128) for h in range(r + 1)]
    sides = (
        (seg == 0, left_h.at[0], lrecv, lb, lenv_o),
        (seg == nseg - 1, right_h.at[pl.ds(0, width)], rrecv, rb, renv_o),
    )
    for which, (edge, own, got, made, dst) in enumerate(sides):

        @pl.when(edge)
        def _():
            pltpu.make_async_copy(own, dst.at[0, 0], sem.at[1 + which]).start()

        @pl.when(jnp.logical_not(edge))
        def _():
            row = ratio_in[which, 0:1]
            a = jnp.sum(jnp.where(lane == 0, row, 0.0), axis=1, keepdims=True)
            b = jnp.sum(jnp.where(lane == 1, row, 0.0), axis=1, keepdims=True)
            weights = (handoff * a * a, handoff * a * b, handoff * b * b)
            for q, (r, h) in enumerate(blocks):
                x = sum(weights[part] * got[part, q].astype(F32) for part in range(3))
                rows, cols = pl.ds(r * 128, 128), pl.ds(h * 128, 128)
                made[rows, cols] = x.astype(BF16)
                if r != h:
                    made[cols, rows] = x.T.astype(BF16)
            pltpu.make_async_copy(made, dst.at[0, 0], sem.at[1 + which]).start()

    out.wait()
    for which, (edge, own, got, made, dst) in enumerate(sides):
        pltpu.make_async_copy(made, dst.at[0, 0], sem.at[1 + which]).wait()


def per_device(
    guess_blocks, onsite_left, onsite_right, hopping_left, hopping_right, sector_dims, kept_dims
):
    n, nseg = lax.axis_size("blk"), lax.axis_size("seg")
    width = guess_blocks.shape[-1]
    half = width // 2
    square, halves = (width, width), (2, width, half)
    count = (width // 128) * (width // 128 + 1) // 2
    forms = (3, count, 128, 128)
    hbm = pl.BlockSpec(memory_space=pltpu.HBM)
    vmem = pl.BlockSpec(memory_space=pltpu.VMEM)
    any_space = pl.BlockSpec(memory_space=pl.ANY)
    smem = pl.BlockSpec(memory_space=pltpu.SMEM)
    dma = pltpu.SemaphoreType.DMA
    scratch = [
        pltpu.VMEM((2,) + square, BF16),
        pltpu.VMEM((2 * width, width), BF16),
        pltpu.VMEM(square, BF16),
        pltpu.VMEM(square, BF16),
        pltpu.VMEM(halves, BF16),
        pltpu.VMEM(square, BF16),
        pltpu.VMEM(halves, F32),
        pltpu.VMEM(halves, F32),
        pltpu.VMEM(halves, F32),
        pltpu.VMEM(halves, F32),
        pltpu.VMEM(halves, BF16),
        pltpu.VMEM((2,) + halves, BF16),
        pltpu.VMEM(halves, BF16),
        pltpu.VMEM((2,) + halves, BF16),
        pltpu.VMEM((width, 2 * width), BF16),
        pltpu.VMEM(square, BF16),
        pltpu.VMEM((width, half), BF16),
        pltpu.VMEM((width, 2 * width), BF16),
        pltpu.VMEM((width, 2 * width), BF16),
        pltpu.VMEM((2 * width, width), BF16),
        pltpu.VMEM((width, 2 * width), BF16),
        pltpu.VMEM(forms, BF16),
        pltpu.VMEM(forms, BF16),
        pltpu.VMEM((8, 128), F32),
        pltpu.VMEM((2, 8, 128), F32),
        pltpu.VMEM((2, n, 128), F32),
        pltpu.SMEM((1, 2), jnp.int32),
        pltpu.SMEM((1, 1), jnp.int32),
        dma((8,)), dma((2,)), dma((2, 2)), dma((2,)), dma((2, 2)), dma((2,)), dma((2,)),
        dma((2,)), dma((2,)), dma((2,)), dma((2,)),
        pltpu.SemaphoreType.REGULAR((2,)),
    ]
    left, right = onsite_left[0, 0], onsite_right[0, 0].reshape(2 * width, width)
    results = pl.pallas_call(
        functools.partial(kernel, n, nseg, width),
        out_shape=(
            pltpu.VMEM(square, F32),
            pltpu.VMEM((8, 128), F32),
            pltpu.VMEM(forms, BF16),
            pltpu.VMEM(forms, BF16),
            pltpu.VMEM((2, 8, 128), F32),
        ),
        in_specs=[hbm] * 7,
        out_specs=(vmem,) * 5,
        scratch_shapes=scratch,
        compiler_params=pltpu.CompilerParams(
            collective_id=0, has_side_effects=True, vmem_limit_bytes=58 * 2**20
        ),
    )(
        guess_blocks[0, 0],
        left,
        right,
        hopping_left[0, 0],
        hopping_right[0, 0],
        sector_dims[0],
        kept_dims,
    )
    return pl.pallas_call(
        functools.partial(store, n, nseg, width),
        out_shape=(
            jax.ShapeDtypeStruct((1, 1) + square, F32),
            jax.ShapeDtypeStruct((1,), F32),
            jax.ShapeDtypeStruct((1, 1) + square, BF16),
            jax.ShapeDtypeStruct((1, 1) + square, BF16),
        ),
        in_specs=[vmem] * 5 + [any_space] * 2,
        out_specs=(any_space, smem, any_space, any_space),
        scratch_shapes=[pltpu.VMEM(square, BF16), pltpu.VMEM(square, BF16), dma((3,))],
        compiler_params=pltpu.CompilerParams(vmem_limit_bytes=4 * 2**20),
    )(*results, left, right)


def solution(mesh):
    in_specs = (
        P("seg", "blk", None, None),
        P("seg", "blk", None, None, None),
        P("seg", "blk", None, None, None),
        P("seg", "blk", None, None),
        P("seg", "blk", None, None),
        P("seg", "blk", None),
        P("seg", "blk"),
    )
    out_specs = (
        P("seg", "blk", None, None),
        P("seg"),
        P("seg", "blk", None, None),
        P("seg", "blk", None, None),
    )
    return jax.shard_map(
        per_device, mesh=mesh, in_specs=in_specs, out_specs=out_specs, check_vma=False
    )
```

```python
import functools
import math

import jax
import jax.numpy as jnp
from jax import lax
from jax.experimental import pallas as pl
from jax.experimental.pallas import tpu as pltpu
from jax.sharding import PartitionSpec as P

ITERS = 4
MESH = pl.DeviceIdType.MESH
F32 = jnp.float32
BF16 = jnp.bfloat16
SIDE = 4
TILE = 256
ROWS = 64
OUTSIDE = 3e38


def dot(a, b):
    return lax.dot_general(a, b, (((1,), (0,)), ((), ())), preferred_element_type=F32)


def dot_nt(a, b):
    return lax.dot_general(a, b, (((1,), (1,)), ((), ())), preferred_element_type=F32)


def fold(x):
    rows, cols = x.shape
    return jnp.sum(x.reshape(rows // 8, 8, cols), axis=0)


def total(x):
    return jnp.sum(jnp.sum(x, axis=0, keepdims=True), axis=1, keepdims=True)


def kernel(
    n, nseg, width,
    guess_h, left_h, right_h, hopl_h, hopr_h, dims_h, kept_h,
    ground_o, energy_o, lrecv, rrecv, ratio_in,
    lv, rv, hl, hlt, hrc, gv, diag, vec, img, acc, cb, xr, cs, cr, pp, rm, qq,
    ff, tt, xx, yy, lsend, rsend, ratio, arsrc, arbuf, dims, kept,
    load_sem, xs_sem, xr_sem, cs_sem, cr_sem, as_sem, ar_sem, env_s, env_r,
    ratio_s, ratio_r, ready,
):
    me = lax.axis_index("blk")
    seg = lax.axis_index("seg")
    right, left = lax.rem(me + 1, n), lax.rem(me + n - 1, n)
    half = width // 2
    hs = (pl.ds(0, half), pl.ds(half, half))
    steps = half // ROWS

    loads = [
        pltpu.make_async_copy(src, dst, load_sem.at[i])
        for i, (src, dst) in enumerate(
            (
                (dims_h, dims),
                (guess_h, gv),
                (hopl_h, hl),
                (hopr_h.at[:, hs[0]], hrc.at[0]),
                (hopr_h.at[:, hs[1]], hrc.at[1]),
                (left_h, lv),
                (right_h, rv),
                (kept_h, kept),
            )
        )
    ]
    for copy in loads:
        copy.start()

    y, z = lax.rem(me, SIDE), me // SIDE
    layers = n // SIDE
    above = lax.rem(z + 1, layers) * SIDE + y
    below = lax.rem(z + layers - 1, layers) * SIDE + y
    barrier = pltpu.get_barrier_semaphore()

    def greet(**device):
        pl.semaphore_signal(barrier, inc=1, device_id=device, device_id_type=MESH)

    for d in range(1, SIDE):
        greet(blk=z * SIDE + lax.rem(y + d, SIDE))
    greet(blk=above)
    greet(blk=below)
    for d in (1, nseg - 1):
        greet(seg=lax.rem(seg + d, nseg))

    @pl.when(y == SIDE - 1)
    def _():
        greet(blk=right)

    @pl.when(y == 0)
    def _():
        greet(blk=left)

    ends = jnp.where(y == SIDE - 1, 1, 0) + jnp.where(y == 0, 1, 0)

    def everyone():
        for _ in range(layers // 2):
            for which, other in ((0, above), (1, below)):
                pl.semaphore_signal(
                    ready.at[which], inc=1, device_id={"blk": other}, device_id_type=MESH
                )
            for which in (0, 1):
                pl.semaphore_wait(ready.at[which], 1)

    loads[0].wait()
    live_rows, live_cols = dims[0, 0], dims[0, 1]

    def live(row0, h, rows):
        i = lax.broadcasted_iota(jnp.int32, (rows, half), 0) + row0
        j = lax.broadcasted_iota(jnp.int32, (rows, half), 1) + h * half
        return (i < live_rows) & (j < live_cols)

    def x_copy(par, h, rc):
        rows = pl.ds(rc * half, half)
        return pltpu.make_async_remote_copy(
            src_ref=cb.at[h, rows], dst_ref=xr.at[par, h, rows],
            send_sem=xs_sem.at[h], recv_sem=xr_sem.at[par, h],
            device_id={"blk": left}, device_id_type=MESH,
        )

    def x_whole(par, h):
        return pltpu.make_async_remote_copy(
            src_ref=cb.at[h], dst_ref=xr.at[par, h],
            send_sem=xs_sem.at[h], recv_sem=xr_sem.at[par, h],
            device_id={"blk": left}, device_id_type=MESH,
        )

    def c_copy(par, h):
        return pltpu.make_async_remote_copy(
            src_ref=cs.at[h], dst_ref=cr.at[par, h],
            send_sem=cs_sem.at[h], recv_sem=cr_sem.at[par, h],
            device_id={"blk": right}, device_id_type=MESH,
        )

    loads[1].wait()

    for h in (0, 1):

        def step(i, _):
            row0 = pl.multiple_of(i * ROWS, ROWS)
            rows = pl.ds(row0, ROWS)
            cb[h, rows] = jnp.where(live(row0, h, ROWS), gv[rows, hs[h]], jnp.zeros((), BF16))
            return 0

        lax.fori_loop(0, width // ROWS, step, 0)

    pl.semaphore_wait(barrier, SIDE - 1 + 4 + ends)
    for h in (0, 1):
        for rc in (0, 1):
            x_copy(0, h, rc).start()

    loads[2].wait()

    @pl.when(me == n - 1)
    def _():
        hl[...] = jnp.zeros_like(hl)

    hlt[...] = hl[...].T
    loads[3].wait()
    loads[4].wait()

    def c_tile(par, h, tile):
        rows = pl.ds(tile * TILE, TILE)
        return pltpu.make_async_remote_copy(
            src_ref=cs.at[h, rows], dst_ref=cr.at[par, h, rows],
            send_sem=cs_sem.at[h], recv_sem=cr_sem.at[par, h],
            device_id={"blk": right}, device_id_type=MESH,
        )

    def couple(par, halves):
        first = halves[0]
        for tile in range(width // TILE):
            rows = pl.ds(tile * TILE, TILE)
            for h in (0, 1):
                rm[rows, hs[h]] = dot(hlt[rows, :], cb[h]).astype(BF16)
            cs[first, rows] = dot(rm[rows, :], hrc[first]).astype(BF16)
            c_tile(par, first, tile).start()
        for h in halves[1:]:
            cs[h] = dot(rm[...], hrc[h]).astype(BF16)
            c_copy(par, h).start()

    def products(k):
        for h in (0, 1):
            pp[:, pl.ds(k * width + h * half, half)] = dot(lv[k], cb[h]).astype(BF16)

    def onsite():
        for h in (0, 1):
            acc[h] = dot(pp[...], rv[:, hs[h]])

    def ar_whole(par):
        return pltpu.make_async_remote_copy(
            src_ref=arbuf.at[par, pl.ds(0, n - 1)], dst_ref=arbuf.at[par, pl.ds(0, n - 1)],
            send_sem=as_sem.at[par], recv_sem=ar_sem.at[par],
            device_id={"blk": right}, device_id_type=MESH,
        )

    lane = lax.broadcasted_iota(jnp.int32, (1, 128), 1)

    def field_sums():
        sums = (jnp.zeros((8, half), F32),) * 3
        for h in (0, 1):

            def step(i, sums):
                corr, weight, cross = sums
                rows = pl.ds(pl.multiple_of(i * ROWS, ROWS), ROWS)
                c = cb[h, rows].astype(F32)
                return (
                    corr + fold(vec[h, rows] * c),
                    weight + fold(c * c),
                    cross + fold(img[h, rows] * c),
                )

            sums = lax.fori_loop(0, width // ROWS, step, sums)
        row = jnp.zeros((1, 128), F32)
        for k in range(3):
            row = jnp.where(lane == k, total(sums[k]), row)
        return row

    def first_half(par, f, row):
        x_whole(par, f).wait_recv()
        qq[...] = dot(hl[...], xr[par, f]).astype(BF16)
        curv = jnp.zeros((8, half), F32)
        for h in (0, 1):
            part = dot_nt(qq[...], hrc[f, hs[h]])
            local = acc[h]
            curv = curv + fold(cb[h].astype(F32) * (local + 2.0 * part))
            acc[h] = local + part
        c_copy(par, 1 - f).wait_recv()
        curv = curv + 2.0 * fold(cb[1 - f].astype(F32) * cr[par, 1 - f].astype(F32))
        row = jnp.where(lane == 3, total(curv), row)
        arsrc[par, 0:1] = row
        arbuf[par, n - 1 : n] = row
        for d in range(1, n):
            pltpu.make_async_remote_copy(
                src_ref=arsrc.at[par, pl.ds(0, 1)], dst_ref=arbuf.at[par, pl.ds(d - 1, 1)],
                send_sem=as_sem.at[par], recv_sem=ar_sem.at[par],
                device_id={"blk": lax.rem(me + d, n)}, device_id_type=MESH,
            ).start()

    def second_half(par, f):
        x_whole(par, 1 - f).wait_recv()
        qq[...] = dot(hl[...], xr[par, 1 - f]).astype(BF16)
        for h in (0, 1):
            acc[h] = acc[h] + dot_nt(qq[...], hrc[1 - f, hs[h]])

    def coefficients(par, start, energy):
        whole = ar_whole(par)
        whole.wait_recv()
        tot = jnp.sum(arbuf[par], axis=0, keepdims=True)
        corr, weight, cross, curv = (
            jnp.sum(jnp.where(lane == k, tot, 0.0), axis=1, keepdims=True) for k in range(4)
        )
        whole.wait_send()
        span = weight - corr * corr
        inverse = 1.0 / span
        slope = cross - corr * energy
        lower = (curv - 2.0 * corr * cross + corr * corr * energy) * inverse
        gap = (energy - lower) / 2.0
        square = slope * slope * inverse
        radius = jnp.sqrt(gap * gap + square)
        keep = radius - gap
        inorm = lax.rsqrt(keep * keep + square)
        scale = -slope * inverse * inorm
        a = keep * inorm - scale * corr
        new = (energy + lower) / 2.0 - radius
        if start is None:
            return a, scale, new
        a = jnp.where(start, 0.0, a)
        scale = jnp.where(start, lax.rsqrt(weight), scale)
        new = jnp.where(start, lower, new)
        return a, scale, new

    def prepare():
        vec[...] = jnp.zeros_like(vec)
        img[...] = jnp.zeros_like(img)
        i = lax.broadcasted_iota(jnp.int32, (128, 128), 0)
        eye = i == lax.broadcasted_iota(jnp.int32, (128, 128), 1)
        for h in (0, 1):
            cols = [
                [
                    jnp.sum(
                        jnp.where(
                            eye,
                            rv[pl.ds(k * width + b, 128), pl.ds(b, 128)].astype(F32),
                            0.0,
                        ),
                        axis=0,
                        keepdims=True,
                    )
                    for b in range(h * half, (h + 1) * half, 128)
                ]
                for k in (0, 1)
            ]
            cols = [jnp.concatenate(c, axis=1) for c in cols]
            for b in range(0, width, 128):
                value = jnp.zeros((128, half), F32)
                for k in (0, 1):
                    block = lv[k, pl.ds(b, 128), pl.ds(b, 128)].astype(F32)
                    col = jnp.sum(jnp.where(eye, block, 0.0), axis=1, keepdims=True)
                    value = value + col * cols[k]
                diag[h, pl.ds(b, 128)] = jnp.where(live(b, h, 128), value, OUTSIDE)

    def update(par, f, last, a, scale, energy):
        for h in (1 - f, f):
            if h is f:
                c_copy(par, f).wait_recv()

            def chunk(rc, _, h=h):
                def step(i, _):
                    rows = pl.ds(pl.multiple_of(rc * half + i * ROWS, ROWS), ROWS)
                    c = cb[h, rows].astype(F32)
                    v = a * vec[h, rows] + scale * c
                    m = a * img[h, rows] + scale * (acc[h, rows] + cr[par, h, rows].astype(F32))
                    vec[h, rows] = v
                    img[h, rows] = m
                    inv = pl.reciprocal(1.0 + jnp.abs(diag[h, rows] - energy), approx=True)
                    cb[h, rows] = ((m - energy * v) * inv).astype(BF16)
                    return 0

                lax.fori_loop(0, steps, step, 0)
                if h is not f:
                    x_copy(1 - par, h, rc).start()
                else:

                    @pl.when(jnp.logical_not(last))
                    def _():
                        x_copy(1 - par, h, rc).start()

                return 0

            lax.fori_loop(0, 2, chunk, 0)

    couple(0, (1, 0))
    loads[5].wait()
    loads[6].wait()
    prepare()

    def iteration(t, energy):
        par = lax.rem(t, 2)
        f = par

        @pl.when(t > 0)
        def _():
            for h in (0, 1):
                c_copy(0, h).wait_send()
            couple(par, (1 - f, f))

        products(0)
        products(1)
        onsite()
        row = field_sums()

        @pl.when(t == 0)
        def _():
            everyone()

        first_half(par, f, row)
        second_half(par, f)
        a, scale, energy = coefficients(par, t == 0, energy)
        for h in (0, 1):
            x_whole(0, h).wait_send()
        update(par, f, t == ITERS - 1, a, scale, energy)
        return energy

    energy = lax.fori_loop(0, ITERS, iteration, jnp.zeros((1, 1), F32))
    par = ITERS % 2
    f = par
    for h in (0, 1):
        c_copy(0, h).wait_send()
    couple(par, (1 - f,))
    products(0)

    loads[7].wait()
    size = kept[0, 0]
    blocks = [(r, h) for r in range(width // 128) for h in range(r + 1)]

    def env_copy(which, part):
        src, dst = ((lsend, lrecv), (rsend, rrecv))[which]
        other = lax.rem(seg + (1, nseg - 1)[which], nseg)
        if part is not None:
            src, dst = src.at[part], dst.at[part]
        return pltpu.make_async_remote_copy(
            src_ref=src, dst_ref=dst, send_sem=env_s.at[which], recv_sem=env_r.at[which],
            device_id={"seg": other}, device_id_type=MESH,
        )

    def ratio_copy(which):
        other = lax.rem(seg + (1, nseg - 1)[which], nseg)
        return pltpu.make_async_remote_copy(
            src_ref=ratio.at[pl.ds(0, 1)], dst_ref=ratio_in.at[which, pl.ds(0, 1)],
            send_sem=ratio_s.at[which], recv_sem=ratio_r.at[which],
            device_id={"seg": other}, device_id_type=MESH,
        )

    sends = (seg < nseg - 1, seg > 0)
    i = lax.broadcasted_iota(jnp.int32, (half, half), 0)
    j = lax.broadcasted_iota(jnp.int32, (half, half), 1)

    def put(send, part, r, h, x):
        x = jnp.where((i + r * half < size) & (j + h * half < size), x, 0.0).astype(BF16)
        for q, (row, col) in enumerate(blocks):
            if row // 2 == r and col // 2 == h:
                b, c = row % 2 * 128, col % 2 * 128
                send[part, q] = x[b : b + 128, c : c + 128]

    quarters = ((0, 0), (1, 0), (1, 1))
    first, second = pl.ds(0, width), pl.ds(width, width)
    for h in (0, 1):
        ff[:, hs[h]] = cb[h]
        ff[:, pl.ds(width + h * half, half)] = vec[h].astype(BF16)
    tt[:, first] = ff[:, first].T
    tt[:, second] = ff[:, second].T
    for h in (0, 1):
        xx[first, hs[h]] = dot(lv[0], ff[:, pl.ds(width + h * half, half)]).astype(BF16)
        yy[:, hs[h]] = dot(ff[:, second], rv[first, hs[h]]).astype(BF16)
    xx[second, :] = pp[:, first]
    for h in (0, 1):
        yy[:, pl.ds(width + h * half, half)] = dot(ff[:, first], rv[first, hs[h]]).astype(BF16)
    everything = pl.ds(0, 2 * width)
    def form(part):
        ours, theirs = ((second, first), (everything, everything), (first, second))[part]
        for r, h in quarters:
            put(lsend, part, r, h, dot(tt[hs[r], ours], xx[theirs, hs[h]]))

        @pl.when(sends[0])
        def _():
            env_copy(0, part).start()

        for r, h in quarters:
            put(rsend, part, r, h, dot_nt(yy[hs[r], theirs], ff[hs[h], ours]))

        @pl.when(sends[1])
        def _():
            env_copy(1, part).start()

    form(0)
    form(1)
    products(1)
    onsite()
    row = field_sums()
    first_half(par, f, row)
    form(2)
    a, scale, energy = coefficients(par, None, energy)
    ratio[...] = jnp.broadcast_to(jnp.where(lane == 0, a, scale), (8, 128))
    for which in (0, 1):

        @pl.when(sends[which])
        def _():
            ratio_copy(which).start()

    energy_o[...] = jnp.broadcast_to(energy, (8, 128))
    for h in (0, 1):

        def step(i, _):
            rows = pl.ds(pl.multiple_of(i * ROWS, ROWS), ROWS)
            v = a * vec[h, rows] + scale * cb[h, rows].astype(F32)
            ground_o[rows, hs[h]] = v * (width * math.sqrt(n))
            return 0

        lax.fori_loop(0, width // ROWS, step, 0)

    for which, receives in ((0, seg > 0), (1, seg < nseg - 1)):

        @pl.when(receives)
        def _():
            env_copy(which, None).wait_recv()
            ratio_copy(which).wait_recv()

    x_whole(0, f).wait_send()
    c_copy(0, 1 - f).wait_send()
    for which in (0, 1):

        @pl.when(sends[which])
        def _():
            env_copy(which, None).wait_send()
            ratio_copy(which).wait_send()


def store(
    n, nseg, width,
    ground, energy, lrecv, rrecv, ratio_in, left_h, right_h,
    ground_o, energy_o, lenv_o, renv_o, lb, rb, sem,
):
    seg = lax.axis_index("seg")
    out = pltpu.make_async_copy(ground, ground_o.at[0, 0], sem.at[0])
    out.start()
    energy_o[0] = energy[0, 0]
    handoff = n * width * math.sqrt(width)
    lane = lax.broadcasted_iota(jnp.int32, (1, 128), 1)
    blocks = [(r, h) for r in range(width // 128) for h in range(r + 1)]
    sides = (
        (seg == 0, left_h.at[0], lrecv, lb, lenv_o),
        (seg == nseg - 1, right_h.at[pl.ds(0, width)], rrecv, rb, renv_o),
    )
    for which, (edge, own, got, made, dst) in enumerate(sides):

        @pl.when(edge)
        def _():
            pltpu.make_async_copy(own, dst.at[0, 0], sem.at[1 + which]).start()

        @pl.when(jnp.logical_not(edge))
        def _():
            row = ratio_in[which, 0:1]
            a = jnp.sum(jnp.where(lane == 0, row, 0.0), axis=1, keepdims=True)
            b = jnp.sum(jnp.where(lane == 1, row, 0.0), axis=1, keepdims=True)
            weights = (handoff * a * a, handoff * a * b, handoff * b * b)
            for q, (r, h) in enumerate(blocks):
                x = sum(weights[part] * got[part, q].astype(F32) for part in range(3))
                rows, cols = pl.ds(r * 128, 128), pl.ds(h * 128, 128)
                made[rows, cols] = x.astype(BF16)
                if r != h:
                    made[cols, rows] = x.T.astype(BF16)
            pltpu.make_async_copy(made, dst.at[0, 0], sem.at[1 + which]).start()

    out.wait()
    for which, (edge, own, got, made, dst) in enumerate(sides):
        pltpu.make_async_copy(made, dst.at[0, 0], sem.at[1 + which]).wait()


def per_device(
    guess_blocks, onsite_left, onsite_right, hopping_left, hopping_right, sector_dims, kept_dims
):
    n, nseg = lax.axis_size("blk"), lax.axis_size("seg")
    width = guess_blocks.shape[-1]
    half = width // 2
    square, halves = (width, width), (2, width, half)
    count = (width // 128) * (width // 128 + 1) // 2
    forms = (3, count, 128, 128)
    hbm = pl.BlockSpec(memory_space=pltpu.HBM)
    vmem = pl.BlockSpec(memory_space=pltpu.VMEM)
    any_space = pl.BlockSpec(memory_space=pl.ANY)
    smem = pl.BlockSpec(memory_space=pltpu.SMEM)
    dma = pltpu.SemaphoreType.DMA
    scratch = [
        pltpu.VMEM((2,) + square, BF16),
        pltpu.VMEM((2 * width, width), BF16),
        pltpu.VMEM(square, BF16),
        pltpu.VMEM(square, BF16),
        pltpu.VMEM(halves, BF16),
        pltpu.VMEM(square, BF16),
        pltpu.VMEM(halves, F32),
        pltpu.VMEM(halves, F32),
        pltpu.VMEM(halves, F32),
        pltpu.VMEM(halves, F32),
        pltpu.VMEM(halves, BF16),
        pltpu.VMEM((2,) + halves, BF16),
        pltpu.VMEM(halves, BF16),
        pltpu.VMEM((2,) + halves, BF16),
        pltpu.VMEM((width, 2 * width), BF16),
        pltpu.VMEM(square, BF16),
        pltpu.VMEM((width, half), BF16),
        pltpu.VMEM((width, 2 * width), BF16),
        pltpu.VMEM((width, 2 * width), BF16),
        pltpu.VMEM((2 * width, width), BF16),
        pltpu.VMEM((width, 2 * width), BF16),
        pltpu.VMEM(forms, BF16),
        pltpu.VMEM(forms, BF16),
        pltpu.VMEM((8, 128), F32),
        pltpu.VMEM((2, 8, 128), F32),
        pltpu.VMEM((2, n, 128), F32),
        pltpu.SMEM((1, 2), jnp.int32),
        pltpu.SMEM((1, 1), jnp.int32),
        dma((8,)), dma((2,)), dma((2, 2)), dma((2,)), dma((2, 2)), dma((2,)), dma((2,)),
        dma((2,)), dma((2,)), dma((2,)), dma((2,)),
        pltpu.SemaphoreType.REGULAR((2,)),
    ]
    left, right = onsite_left[0, 0], onsite_right[0, 0].reshape(2 * width, width)
    results = pl.pallas_call(
        functools.partial(kernel, n, nseg, width),
        out_shape=(
            pltpu.VMEM(square, F32),
            pltpu.VMEM((8, 128), F32),
            pltpu.VMEM(forms, BF16),
            pltpu.VMEM(forms, BF16),
            pltpu.VMEM((2, 8, 128), F32),
        ),
        in_specs=[hbm] * 7,
        out_specs=(vmem,) * 5,
        scratch_shapes=scratch,
        compiler_params=pltpu.CompilerParams(
            collective_id=0, has_side_effects=True, vmem_limit_bytes=58 * 2**20
        ),
    )(
        guess_blocks[0, 0],
        left,
        right,
        hopping_left[0, 0],
        hopping_right[0, 0],
        sector_dims[0],
        kept_dims,
    )
    return pl.pallas_call(
        functools.partial(store, n, nseg, width),
        out_shape=(
            jax.ShapeDtypeStruct((1, 1) + square, F32),
            jax.ShapeDtypeStruct((1,), F32),
            jax.ShapeDtypeStruct((1, 1) + square, BF16),
            jax.ShapeDtypeStruct((1, 1) + square, BF16),
        ),
        in_specs=[vmem] * 5 + [any_space] * 2,
        out_specs=(any_space, smem, any_space, any_space),
        scratch_shapes=[pltpu.VMEM(square, BF16), pltpu.VMEM(square, BF16), dma((3,))],
        compiler_params=pltpu.CompilerParams(vmem_limit_bytes=4 * 2**20),
    )(*results, left, right)


def solution(mesh):
    in_specs = (
        P("seg", "blk", None, None),
        P("seg", "blk", None, None, None),
        P("seg", "blk", None, None, None),
        P("seg", "blk", None, None),
        P("seg", "blk", None, None),
        P("seg", "blk", None),
        P("seg", "blk"),
    )
    out_specs = (
        P("seg", "blk", None, None),
        P("seg"),
        P("seg", "blk", None, None),
        P("seg", "blk", None, None),
    )
    return jax.shard_map(
        per_device, mesh=mesh, in_specs=in_specs, out_specs=out_specs, check_vma=False
    )
```
